256 devices in a mesh: seq: 64 (over z, x, core), head: 4 (over y).
Axes of the slice: x: 4, y: 4, z: 8, core: 2. Of those that a mesh axis runs over, the one named last changes fastest.
Arguments:
- query_vectors: bfloat16 [8192, 4096], P('seq', 'head'), may hold values from -6 to 6
- key_vectors: bfloat16 [8192, 4096], P('seq', 'head'), may hold values from -6 to 6
- value_vectors: bfloat16 [8192, 4096], P('seq', 'head'), may hold values from -6 to 6
- log_decay: float32 [32, 8192], P('head', 'seq'), may hold values from -1.5 to 0, as said below
- write_strength: float32 [32, 8192], P('head', 'seq'), may hold values from 0 to 1, as said below
- output_gate: bfloat16 [8192, 4096], P('seq', 'head'), may hold values from -6 to 6
- norm_gain: float32 [128], replicated, may hold values from 0.1 to 1.9
- out_proj: bfloat16 [4096, 2304], P('head'), may hold values from -0.09375 to 0.09375
Outputs:
- mixed: bfloat16 [8192, 2304], P(('seq', 'head'))
The draws below stay inside these ranges and needn't reach their ends.
Inputs may be any that keep to these rules, and one draw needn't show every extreme that they name: `log_decay`: every entry is at most zero. `write_strength`: every entry is positive.
All inputs are finite; a program needn't handle non-finite values.
Results may differ from the reference program's by a relative error of at most 0.015.
Values may be sent and summed in bfloat16 or wider, within the bound.
A program may use at most 192 MiB of HBM per device.

```python
import jax
import jax.numpy as jnp
from jax import lax

D = 2304
HEADS = 32
KD = 128
DV = 128
GROUP = 64
TOK_DEV = 128
TOKENS = 8192


def slow_heads(key, tenth_parts):
    return jax.random.randint(jax.random.fold_in(key, 101), (HEADS, 1), 0, 10) < tenth_parts


def draw_log_decay(key, part):
    slow = slow_heads(key, 5)
    key = jax.random.fold_in(key, 1)
    keys = jax.random.split(key, 6)
    rough = jax.random.uniform(keys[0], (HEADS, TOKENS), jnp.float32, 0.5, 1.5)
    levels = jnp.exp(jax.random.uniform(keys[1], (HEADS, TOKENS // TOK_DEV), jnp.float32, -0.5, 0.5))
    levels = jnp.repeat(levels, TOK_DEV, axis=1)
    slow_rate = jax.random.uniform(keys[2], (HEADS, 1), jnp.float32, 0.2, 0.6) / TOKENS
    fast_rate = 1.0 / jax.random.uniform(keys[3], (HEADS, 1), jnp.float32, 30.0, 50.0)
    forgetting_speed = jnp.where(slow, slow_rate, fast_rate) * rough * levels
    spots = jax.random.randint(keys[4], (HEADS, 2, 1), 0, TOKENS)
    stack_position = jnp.log(jax.random.uniform(keys[5], (HEADS, 2, 1), jnp.float32, 0.5, 0.8))
    agreeing_tally = jnp.arange(TOKENS)[None, None, :] == spots
    token_clusters = jnp.sum(jnp.where(agreeing_tally, stack_position, 0.0), axis=1)
    return (token_clusters - forgetting_speed).astype(jnp.float32)


def draw_write_strength(key, part):
    slow = slow_heads(key, 5)
    key = jax.random.fold_in(key, 2)
    keys = jax.random.split(key, 3)
    rough = jax.random.uniform(keys[0], (HEADS, TOKENS), jnp.float32, 0.5, 1.5)
    sluggish_level = jax.random.uniform(keys[1], (HEADS, 1), jnp.float32, 0.25, 0.6) * KD / TOKENS
    fast_level = jax.random.uniform(keys[2], (HEADS, 1), jnp.float32, 0.2, 0.6)
    return (jnp.where(slow, sluggish_level, fast_level) * rough).astype(jnp.float32)


def shard_levels(stream_key, dims, cuts, low, top_value):
    def one(axis_at, parts):
        heights = jax.random.uniform(jax.random.fold_in(jax.random.fold_in(stream_key, 6), axis_at), (parts,), jnp.float32, low / len(cuts), top_value / len(cuts))
        return jnp.repeat(jnp.exp(heights), dims[axis_at] // parts).reshape((-1,) + (1,) * (len(dims) - axis_at - 1))

    level = one(*cuts[0])
    for cut in cuts[1:]:
        level = level * one(*cut)
    return level


def bell_draw(own_key, dims, scale, bound, cuts=(), kind=jnp.bfloat16):
    level = shard_levels(own_key, dims, cuts, -0.22, 0.18) if cuts else 1.0
    drawn = jax.random.normal(own_key, dims, jnp.float32) * scale * level
    return jnp.minimum(jnp.maximum(drawn, -bound), bound).astype(kind)


def setup_inputs(seed: int = 0) -> dict:
    arg_keys = jax.random.split(jax.random.key(seed), 9)
    query_vectors = bell_draw(arg_keys[0], (TOKENS, HEADS * KD), 1.0, 6.0, ((0, 64), (1, 4)))
    key_vectors = bell_draw(arg_keys[1], (TOKENS, HEADS * KD), 1.0, 6.0, ((0, 64), (1, 4)))
    value_vectors = bell_draw(arg_keys[2], (TOKENS, HEADS * DV), 1.0, 6.0, ((0, 64), (1, 4)))
    log_decay = draw_log_decay(jax.random.fold_in(arg_keys[8], 71), 0)
    write_strength = draw_write_strength(jax.random.fold_in(arg_keys[8], 71), 0)
    output_gate = bell_draw(arg_keys[5], (TOKENS, HEADS * DV), 1.0, 6.0, ((0, 64), (1, 4)))
    norm_gain = jnp.clip(1.0 + 0.18 * jax.random.normal(arg_keys[6], (DV,), jnp.float32), 0.1, 1.9)
    out_proj = bell_draw(arg_keys[7], (HEADS * DV, D), (HEADS * DV) ** -0.5, 0.09375, ((0, 4),))
    return dict(query_vectors=query_vectors, key_vectors=key_vectors, value_vectors=value_vectors, log_decay=log_decay, write_strength=write_strength, output_gate=output_gate, norm_gain=norm_gain, out_proj=out_proj)


HIGH = lax.Precision.HIGHEST

def dot_high(left, right):
    return jnp.dot(left.astype(jnp.float32), right.astype(jnp.float32), precision=HIGH, preferred_element_type=jnp.float32)

def group_terms(query, keyrow, value, decay, strength):
    width = keyrow.shape[1]
    vwidth = value.shape[1]
    length = keyrow.shape[0]
    query = query * lax.rsqrt(lax.optimization_barrier(jnp.sum(query * query, axis=1, keepdims=True)) + 1e-06)
    keyrow = keyrow * lax.rsqrt(lax.optimization_barrier(jnp.sum(keyrow * keyrow, axis=1, keepdims=True)) + 1e-06)
    cumul = jnp.cumsum(decay)
    spread = cumul[:, None] - cumul[None, :]
    places = jnp.arange(length)
    lower = places[:, None] >= places[None, :]
    strict = places[:, None] > places[None, :]
    ratio = jnp.where(lower, jnp.exp(jnp.minimum(spread, 0.0)), 0.0)
    couple = strength[:, None] * jnp.where(strict, ratio, 0.0) * dot_high(keyrow, keyrow.T)
    growth = jnp.exp(cumul)
    rhs = strength[:, None] * jnp.concatenate([value, growth[:, None] * keyrow], axis=1)
    solved = jax.scipy.linalg.solve_triangular(jnp.eye(length, dtype=jnp.float32) + couple, rhs, lower=True, unit_diagonal=True)
    score_values = ratio * dot_high(query, keyrow.T)
    both = dot_high(score_values, solved)
    tail = jnp.exp(cumul[-1] - cumul)
    ends = dot_high((tail[:, None] * keyrow).T, solved)
    transit = growth[-1] * jnp.eye(width, dtype=jnp.float32) - ends[:, vwidth:]
    inject = ends[:, :vwidth]
    reach = growth[:, None] * query - both[:, vwidth:]
    local = both[:, :vwidth]
    return (transit, inject, reach, local)

def reference(query_vectors, key_vectors, value_vectors, log_decay, write_strength, output_gate, norm_gain, out_proj):
    blocks = TOKENS // GROUP

    def heads_first(whole, width):
        return whole.reshape(TOKENS, HEADS, width).transpose(1, 0, 2)

    def one_head(items):
        query, keyrow, value, decay, strength = items

        def cut(array, width):
            return array.astype(jnp.float32).reshape(blocks, GROUP, width)
        transit, inject, reach, local = jax.vmap(group_terms)(cut(query, KD), cut(keyrow, KD), cut(value, DV), decay.reshape(blocks, GROUP), strength.reshape(blocks, GROUP))

        def advance(state, item):
            tr_mat, input_matrix, re_mat, lo_mat = item
            output = dot_high(re_mat, state) + lo_mat
            return (dot_high(tr_mat, state) + input_matrix, output)
        _, outputs = lax.scan(advance, jnp.zeros((KD, DV), jnp.float32), (transit, inject, reach, local))
        return outputs.reshape(TOKENS, DV)
    head_out = lax.map(one_head, (heads_first(query_vectors, KD), heads_first(key_vectors, KD), heads_first(value_vectors, DV), log_decay, write_strength))
    outputs = head_out.transpose(1, 0, 2)
    square = lax.optimization_barrier(jnp.mean(outputs * outputs, axis=2, keepdims=True))
    gating = jax.nn.sigmoid(output_gate.astype(jnp.float32).reshape(TOKENS, HEADS, DV))
    rescaled_heads = (outputs * lax.rsqrt(square + 1e-06) * norm_gain * gating).astype(jnp.bfloat16).reshape(TOKENS, HEADS * DV)
    mixed = jnp.dot(rescaled_heads.astype(jnp.float32), out_proj.astype(jnp.float32), precision=HIGH, preferred_element_type=jnp.float32)
    return mixed.astype(jnp.bfloat16)
```

```python
import jax
import jax.numpy as jnp
from jax import lax
from jax.experimental import pallas as pl
from jax.experimental.pallas import tpu as pltpu
from jax.sharding import PartitionSpec as P

MESH = pl.DeviceIdType.MESH
F32 = jnp.float32
BF16 = jnp.bfloat16

ROW = 8
DEEP = 8
FANS = 4
HEADS = 8
N = 128
GROWS = 16
MSG = GROWS + 2 * N
CHUNKS = 3
EPS = 1e-06


def bdot(left, right, dims):
    return lax.dot_general(
        left.astype(BF16), right.astype(BF16), (dims, ((0,), (0,))), preferred_element_type=F32
    )


NN = ((2,), (1,))
NT = ((2,), (2,))
TN = ((1,), (1,))


def split(x):
    high = x.astype(BF16)
    return high, (x - high.astype(F32)).astype(BF16)


def bdot_left(left, right, dims=NN):
    high, low = split(left)
    return bdot(high, right, dims) + bdot(low, right, dims)


def bdot_right(left, right, dims=NN):
    high, low = split(right)
    return bdot(left, high, dims) + bdot(left, low, dims)


def bdot_both(left, right, dims=NN):
    lh, ll = split(left)
    rh, rl = split(right)
    return bdot(lh, rh, dims) + (bdot(lh, rl, dims) + bdot(ll, rh, dims))


def dot(left, right):
    return jnp.dot(left.astype(BF16), right.astype(BF16), preferred_element_type=F32)


def dot_left(left, right):
    high, low = split(left)
    return dot(high, right) + dot(low, right)


def inverse(couple, row, col):
    def level(size):
        pair = (row // (2 * size)) == (col // (2 * size))
        return pair & ((row // size) % 2 == 1) & ((col // size) % 2 == 0)

    eye = jnp.where(row == col, 1.0, 0.0).astype(F32)
    solved = eye - jnp.where(level(1), couple, 0.0)
    size = 2
    while size < N:
        below = jnp.where(level(size), couple, 0.0)
        solved = solved - bdot(solved, bdot(below, solved, NN), NN)
        size *= 2
    rest = (eye - solved) - bdot_both(couple, solved)
    return solved + bdot(solved, rest, NN)


def local_terms(query, keyrow, value, cum_row, cum_col, str_row, str_col):
    shape = query.shape
    row = lax.broadcasted_iota(jnp.int32, shape, 1)
    col = lax.broadcasted_iota(jnp.int32, shape, 2)
    keykey = bdot(keyrow, keyrow, NT)
    diag = jnp.where(row == col, keykey, 0.0)
    kscale_row = lax.rsqrt(jnp.sum(diag, axis=1, keepdims=True) + EPS)
    kscale_col = lax.rsqrt(jnp.sum(diag, axis=2, keepdims=True) + EPS)
    ratio = jnp.where(row >= col, jnp.exp(jnp.minimum(cum_col - cum_row, 0.0)), 0.0) * kscale_row
    couple = jnp.where(row > col, ratio * keykey, 0.0) * (str_col * kscale_col)
    solved = inverse(couple, row, col)
    from_value = bdot_left(solved * str_row, value)
    from_key = bdot_left(solved * (str_row * jnp.exp(cum_row) * kscale_row), keyrow)
    both = jnp.concatenate([from_key, from_value], axis=2)
    last = cum_row[:, :, N - 1 :]
    tail = jnp.exp(last - cum_col) * kscale_col
    ends = bdot_right(keyrow, both * tail, TN)
    return ratio, both, ends, jnp.exp(last)


def local_reads(query, keyrow, ratio, both, cum_col):
    query32 = query.astype(F32)
    qscale = lax.rsqrt(jnp.sum(query32 * query32, axis=2, keepdims=True) + EPS)
    score = ratio * bdot(query, keyrow, NT) * qscale
    read = bdot_both(score, both)
    reach = query32 * (jnp.exp(cum_col) * qscale) - read[:, :, :N]
    return reach, read[:, :, N:]


def decay_rows(gain):
    place = lax.broadcasted_iota(jnp.int32, (GROWS, N), 0)
    high = gain.astype(BF16).astype(F32)
    middle = (gain - high).astype(BF16).astype(F32)
    low = gain - high - middle
    rows = jnp.where(place == 0, high, jnp.where(place == 1, middle, jnp.where(place == 2, low, 0.0)))
    return rows.astype(BF16)


def read_message(buffer, index):
    gain = jnp.sum(buffer[index, :GROWS, :].astype(F32), axis=0, keepdims=True)
    return gain, buffer[index, GROWS : GROWS + N, :], buffer[index, GROWS + N :, :]


def kernel(
    q_ref,
    k_ref,
    v_ref,
    decay_ref,
    strength_ref,
    gain_ref,
    gate_any,
    proj_any,
    out_ref,
    gate_buf,
    proj_buf,
    head_send,
    head_recv,
    pre_d,
    pre_j,
    pre_g,
    total_buf,
    state_send,
    state_recv,
    reach_buf,
    local_buf,
    normed_buf,
    part_buf,
    part_recv,
    load_sem,
    hs_sem,
    hr_sem,
    rs_sem,
    rr_sem,
    ls_sem,
    lr_sem,
    ss_sem,
    sr_sem,
    ps_sem,
    pr_sem,
):
    place = lax.axis_index("seq")
    fan = lax.axis_index("head")
    deep = place // ROW
    mine = lax.rem(place, ROW)
    right = lax.rem(deep + 1, DEEP)
    left = lax.rem(deep + DEEP - 1, DEEP)
    row_peers = [lax.rem(mine + step, ROW) for step in range(1, ROW)]
    fan_peers = [lax.rem(fan + step, FANS) for step in (2, 1, 3)]

    loads = [
        pltpu.make_async_copy(gate_any, gate_buf, load_sem.at[0]),
        pltpu.make_async_copy(proj_any, proj_buf, load_sem.at[1]),
    ]
    for load in loads:
        load.start()

    barrier = pltpu.get_barrier_semaphore()
    greeted = [(deep * ROW + peer, fan) for peer in row_peers]
    greeted += [(right * ROW + mine, fan), (left * ROW + mine, fan)]
    greeted += [(place, peer) for peer in fan_peers]
    for device in greeted:
        pl.semaphore_signal(barrier, inc=1, device_id=device, device_id_type=MESH)

    def remote(source, target, send, recv, device):
        return pltpu.make_async_remote_copy(
            src_ref=source,
            dst_ref=target,
            send_sem=send,
            recv_sem=recv,
            device_id=device,
            device_id_type=MESH,
        )

    tri_row = lax.broadcasted_iota(jnp.int32, (N, N), 0)
    tri_col = lax.broadcasted_iota(jnp.int32, (N, N), 1)
    upper = jnp.where(tri_row <= tri_col, 1.0, 0.0).astype(F32)
    strength = strength_ref[...]
    cumul = jnp.dot(
        decay_ref[...], upper, precision=lax.Precision.HIGHEST, preferred_element_type=F32
    )
    turned = jnp.concatenate([cumul, strength, jnp.zeros((N - 2 * HEADS, N), F32)], axis=0).T
    heads = range(HEADS)
    cum_row = jnp.stack([cumul[h : h + 1, :] for h in heads])
    str_row = jnp.stack([strength[h : h + 1, :] for h in heads])
    cum_col = jnp.stack([turned[:, h : h + 1] for h in heads])
    str_col = jnp.stack([turned[:, HEADS + h : HEADS + h + 1] for h in heads])
    query, keyrow, value = (
        jnp.stack([ref[:, h * N : (h + 1) * N] for h in heads]) for ref in (q_ref, k_ref, v_ref)
    )
    ratio, both, ends, last = local_terms(
        query, keyrow, value, cum_row, cum_col, str_row, str_col
    )
    head_send[:, GROWS : GROWS + N, :] = (-ends[:, :, :N]).astype(BF16)
    head_send[:, GROWS + N :, :] = ends[:, :, N:].astype(BF16)
    for h in heads:
        head_send[h, :GROWS, :] = decay_rows(jnp.broadcast_to(last[h], (GROWS, N)))

    pl.semaphore_wait(barrier, len(greeted))
    head_copies = [
        remote(
            head_send.at[peer],
            head_recv.at[mine],
            hs_sem.at[peer],
            hr_sem.at[mine],
            (deep * ROW + peer, fan),
        )
        for peer in row_peers
    ]
    for copy in head_copies:
        copy.start()
    head_recv[mine] = head_send[mine]

    reach, local = local_reads(query, keyrow, ratio, both, cum_col)
    reach_buf[...] = reach
    local_buf[...] = local

    for i in range(ROW):

        @pl.when(mine != i)
        def _():
            remote(
                head_send.at[i], head_recv.at[i], hs_sem.at[i], hr_sem.at[i], (deep * ROW + i, fan)
            ).wait_recv()

    gains = jnp.ones((1, N), F32)
    run_d = jnp.zeros((N, N), F32)
    run_j = jnp.zeros((N, N), F32)
    for i in range(ROW):
        pre_g[i] = jnp.broadcast_to(gains, (8, N))
        pre_d[pl.ds(i * N, N), :] = run_d.astype(BF16)
        pre_j[i] = run_j
        gain, step_d, step_j = read_message(head_recv, i)
        if i == 0:
            run_d, run_j = step_d.astype(F32), step_j.astype(F32)
        else:
            high, low = split(jnp.concatenate([run_d, run_j], axis=1))
            prod = dot(step_d, high) + dot(step_d, low)
            run_d = gain * run_d + gains * step_d.astype(F32) + prod[:, :N]
            run_j = gain * run_j + step_j.astype(F32) + prod[:, N:]
        gains = gains * gain
    total_buf[deep, :GROWS, :] = decay_rows(jnp.broadcast_to(gains, (GROWS, N)))
    total_buf[deep, GROWS : GROWS + N, :] = run_d.astype(BF16)
    total_buf[deep, GROWS + N :, :] = run_j.astype(BF16)

    half = DEEP // 2

    def ring(step, sign, send, recv):
        slot = lax.rem(deep + DEEP - sign * (step - 1), DEEP)
        to = right if sign > 0 else left
        return remote(
            total_buf.at[slot],
            total_buf.at[slot],
            send.at[step - 1],
            recv.at[step - 1],
            (to * ROW + mine, fan),
        )

    def arrived(step, sign, send, recv):
        slot = lax.rem(deep + DEEP - sign * step, DEEP)
        remote(
            total_buf.at[slot],
            total_buf.at[slot],
            send.at[step - 1],
            recv.at[step - 1],
            ((left if sign > 0 else right) * ROW + mine, fan),
        ).wait_recv()
        return slot

    rings = [ring(1, 1, rs_sem, rr_sem), ring(1, -1, ls_sem, lr_sem)]
    for copy in rings:
        copy.start()
    near_g = jnp.ones((1, N), F32)
    near_d = jnp.zeros((N, N), F32)
    near_j = jnp.zeros((N, N), F32)
    far = jnp.zeros((N, N), F32)
    for step in range(1, half + 1):
        slot = arrived(step, 1, rs_sem, rr_sem)
        if step < half:
            copy = ring(step + 1, 1, rs_sem, rr_sem)
            copy.start()
            rings.append(copy)
        if step < half:
            far_slot = arrived(step, -1, ls_sem, lr_sem)
            if step < half - 1:
                copy = ring(step + 1, -1, ls_sem, lr_sem)
                copy.start()
                rings.append(copy)
        gain, step_d, step_j = read_message(total_buf, slot)
        valid = deep >= step
        gain = jnp.where(valid, gain, 1.0)
        step_d = jnp.where(valid, step_d.astype(F32), 0.0)
        step_j = jnp.where(valid, step_j.astype(F32), 0.0)
        prod = dot_left(near_d, jnp.concatenate([step_d, step_j], axis=1))
        near_j = near_j + near_g * step_j + prod[:, N:]
        near_d = near_g * step_d + gain * near_d + prod[:, :N]
        near_g = near_g * gain
        if step < half:
            gain, step_d, step_j = read_message(total_buf, far_slot)
            high, low = split(far)
            moved = gain * far + dot(step_d, high) + dot(step_d, low) + step_j.astype(F32)
            far = jnp.where(deep + step >= DEEP, moved, far)
    state = near_g * far + dot_left(near_d, far) + near_j

    starts = dot(pre_d[...], state)
    for i in range(ROW):
        first = pre_g[i, :1, :] * state + starts[i * N : (i + 1) * N] + pre_j[i]
        state_send[i] = first.astype(BF16)
    state_copies = [
        remote(
            state_send.at[peer],
            state_recv.at[mine],
            ss_sem.at[peer],
            sr_sem.at[mine],
            (deep * ROW + peer, fan),
        )
        for peer in row_peers
    ]
    for copy in state_copies:
        copy.start()
    state_recv[mine] = state_send[mine]
    loads[0].wait()
    gating = jax.nn.sigmoid(gate_buf[...].astype(F32)) * jnp.tile(gain_ref[...], (1, HEADS))
    for peer in row_peers:
        remote(
            state_send.at[peer],
            state_recv.at[peer],
            ss_sem.at[peer],
            sr_sem.at[peer],
            (deep * ROW + peer, fan),
        ).wait_recv()
    outputs = bdot_left(reach_buf[...], state_recv[...]) + local_buf[...]
    square = jnp.mean(outputs * outputs, axis=2, keepdims=True)
    outputs = outputs * lax.rsqrt(square + EPS)
    for h in heads:
        columns = slice(h * N, (h + 1) * N)
        normed_buf[:, columns] = (outputs[h] * gating[:, columns]).astype(BF16)

    loads[1].wait()
    rows = N // FANS
    width = proj_buf.shape[1] // CHUNKS
    part_copies = []
    for c in range(CHUNKS):
        part_buf[c] = jnp.dot(
            normed_buf[...],
            proj_buf[:, c * width : (c + 1) * width],
            preferred_element_type=F32,
        ).astype(BF16)
        for n, peer in enumerate(fan_peers):
            copy = remote(
                part_buf.at[c, pl.ds(pl.multiple_of(peer * rows, rows), rows), :],
                part_recv.at[c, fan],
                ps_sem.at[c, n],
                pr_sem.at[c, fan],
                (place, peer),
            )
            copy.start()
            part_copies.append(copy)
        part_recv[c, fan] = part_buf[c, pl.ds(pl.multiple_of(fan * rows, rows), rows), :]
    for c in range(CHUNKS):
        for n, peer in enumerate(fan_peers):
            remote(
                part_buf.at[c, pl.ds(pl.multiple_of(peer * rows, rows), rows), :],
                part_recv.at[c, peer],
                ps_sem.at[c, n],
                pr_sem.at[c, peer],
                (place, peer),
            ).wait_recv()
        summed = part_recv[c, 0].astype(F32)
        for n in range(1, FANS):
            summed = summed + part_recv[c, n].astype(F32)
        out_ref[:, c * width : (c + 1) * width] = summed.astype(BF16)

    for copy in head_copies + rings + state_copies + part_copies:
        copy.wait_send()


def on_device(
    query_vectors,
    key_vectors,
    value_vectors,
    log_decay,
    write_strength,
    output_gate,
    norm_gain,
    out_proj,
):
    rows, wide = query_vectors.shape
    depth, width = out_proj.shape
    vmem = pl.BlockSpec(memory_space=pltpu.VMEM)
    anywhere = pl.BlockSpec(memory_space=pl.ANY)
    dma = pltpu.SemaphoreType.DMA
    half = DEEP // 2
    return pl.pallas_call(
        kernel,
        out_shape=jax.ShapeDtypeStruct((rows // FANS, width), BF16),
        in_specs=[vmem] * 6 + [anywhere] * 2,
        out_specs=vmem,
        scratch_shapes=[
            pltpu.VMEM((rows, wide), BF16),
            pltpu.VMEM((depth, width), BF16),
            pltpu.VMEM((HEADS, MSG, N), BF16),
            pltpu.VMEM((ROW, MSG, N), BF16),
            pltpu.VMEM((ROW * N, N), BF16),
            pltpu.VMEM((ROW, N, N), F32),
            pltpu.VMEM((ROW, 8, N), F32),
            pltpu.VMEM((DEEP, MSG, N), BF16),
            pltpu.VMEM((ROW, N, N), BF16),
            pltpu.VMEM((HEADS, N, N), BF16),
            pltpu.VMEM((HEADS, N, N), F32),
            pltpu.VMEM((HEADS, N, N), F32),
            pltpu.VMEM((rows, wide), BF16),
            pltpu.VMEM((CHUNKS, rows, width // CHUNKS), BF16),
            pltpu.VMEM((CHUNKS, FANS, rows // FANS, width // CHUNKS), BF16),
            dma((2,)),
            dma((HEADS,)),
            dma((ROW,)),
            dma((half,)),
            dma((half,)),
            dma((half - 1,)),
            dma((half - 1,)),
            dma((ROW,)),
            dma((HEADS,)),
            dma((CHUNKS, FANS - 1)),
            dma((CHUNKS, FANS)),
        ],
        compiler_params=pltpu.CompilerParams(
            collective_id=0, has_side_effects=True, vmem_limit_bytes=50 * 1024 * 1024
        ),
        cost_estimate=pl.CostEstimate(
            flops=2_000_000_000, bytes_accessed=6_000_000, transcendentals=500_000
        ),
    )(
        query_vectors,
        key_vectors,
        value_vectors,
        log_decay,
        write_strength,
        norm_gain.reshape(1, N),
        output_gate,
        out_proj,
    )


def solution(mesh):
    in_specs = (
        P("seq", "head"),
        P("seq", "head"),
        P("seq", "head"),
        P("head", "seq"),
        P("head", "seq"),
        P("seq", "head"),
        P(),
        P("head", None),
    )
    out_specs = P(("seq", "head"), None)
    return jax.shard_map(
        on_device, mesh=mesh, in_specs=in_specs, out_specs=out_specs, check_vma=False
    )
```

```python
import jax
import jax.numpy as jnp
from jax import lax
from jax.experimental import pallas as pl
from jax.experimental.pallas import tpu as pltpu
from jax.sharding import PartitionSpec as P

MESH = pl.DeviceIdType.MESH
F32 = jnp.float32
BF16 = jnp.bfloat16

ROW = 8
GROUP = 16
GROUPS = 4
FANS = 4
HEADS = 8
BATCH = 4
N = 128
GROWS = 16
MSG = GROWS + 2 * N
CHUNKS = 3
OWNERS = tuple(ROW * ((h % 4 + h // 4 + 1) % 2) + 2 * (h % 4) for h in range(HEADS))
EPS = 1e-06


def bdot(left, right, dims):
    return lax.dot_general(
        left.astype(BF16), right.astype(BF16), (dims, ((0,), (0,))), preferred_element_type=F32
    )


NN = ((2,), (1,))
NT = ((2,), (2,))
TN = ((1,), (1,))


def split(x):
    high = x.astype(BF16)
    return high, (x - high.astype(F32)).astype(BF16)


def bdot_left(left, right, dims=NN):
    high, low = split(left)
    return bdot(high, right, dims) + bdot(low, right, dims)


def bdot_right(left, right, dims=NN):
    high, low = split(right)
    return bdot(left, high, dims) + bdot(left, low, dims)


def bdot_both(left, right, dims=NN):
    lh, ll = split(left)
    rh, rl = split(right)
    return bdot(lh, rh, dims) + (bdot(lh, rl, dims) + bdot(ll, rh, dims))


def dot(left, right):
    return jnp.dot(left.astype(BF16), right.astype(BF16), preferred_element_type=F32)


def dot_left(left, right):
    high, low = split(left)
    return dot(high, right) + dot(low, right)


def dot_right(left, right):
    high, low = split(right)
    return dot(left, high) + dot(left, low)


def dot_both(left, right):
    lh, ll = split(left)
    rh, rl = split(right)
    return dot(lh, rh) + (dot(lh, rl) + dot(ll, rh))


def inverse(couple, row, col):
    def level(size):
        pair = (row // (2 * size)) == (col // (2 * size))
        return pair & ((row // size) % 2 == 1) & ((col // size) % 2 == 0)

    eye = jnp.where(row == col, 1.0, 0.0).astype(F32)
    solved = eye - jnp.where(level(1), couple, 0.0)
    size = 2
    while size < N:
        below = jnp.where(level(size), couple, 0.0)
        solved = solved - bdot(solved, bdot(below, solved, NN), NN)
        size *= 2
    rest = (eye - solved) - bdot_both(couple, solved)
    return solved + bdot(solved, rest, NN)


def local_terms(keyrow, value, cum_row, cum_col, str_row, str_col):
    shape = keyrow.shape
    row = lax.broadcasted_iota(jnp.int32, shape, 1)
    col = lax.broadcasted_iota(jnp.int32, shape, 2)
    keykey = bdot(keyrow, keyrow, NT)
    diag = jnp.where(row == col, keykey, 0.0)
    kscale_row = lax.rsqrt(jnp.sum(diag, axis=1, keepdims=True) + EPS)
    kscale_col = lax.rsqrt(jnp.sum(diag, axis=2, keepdims=True) + EPS)
    ratio = jnp.where(row >= col, jnp.exp(jnp.minimum(cum_col - cum_row, 0.0)), 0.0) * kscale_row
    couple = jnp.where(row > col, ratio * keykey, 0.0) * (str_col * kscale_col)
    solved = inverse(couple, row, col)
    from_value = bdot_left(solved * str_row, value)
    from_key = bdot_left(solved * (str_row * jnp.exp(cum_row) * kscale_row), keyrow)
    both = jnp.concatenate([from_key, from_value], axis=2)
    last = cum_row[:, :, N - 1 :]
    tail = jnp.exp(last - cum_col) * kscale_col
    ends = bdot_right(keyrow, both * tail, TN)
    return ratio, both, ends, jnp.exp(last)


def local_reads(query, keyrow, ratio, both, cum_col):
    query32 = query.astype(F32)
    qscale = lax.rsqrt(jnp.sum(query32 * query32, axis=2, keepdims=True) + EPS)
    score = ratio * bdot(query, keyrow, NT) * qscale
    read = bdot_both(score, both)
    reach = query32 * (jnp.exp(cum_col) * qscale) - read[:, :, :N]
    return reach, read[:, :, N:]


def decay_rows(gain):
    place = lax.broadcasted_iota(jnp.int32, (GROWS, N), 0)
    high = gain.astype(BF16).astype(F32)
    middle = (gain - high).astype(BF16).astype(F32)
    low = gain - high - middle
    rows = jnp.where(place == 0, high, jnp.where(place == 1, middle, jnp.where(place == 2, low, 0.0)))
    return rows.astype(BF16)


def read_message(buffer, index):
    gain = jnp.sum(buffer[index, N : N + GROWS, :].astype(F32), axis=0, keepdims=True)
    return gain, buffer[index, N + GROWS :, :], buffer[index, :N, :]


def advance(run, step):
    run_g, run_d, run_j = run
    step_g, step_d, step_j = step
    prod = dot_right(step_d, jnp.concatenate([run_d, run_j], axis=1))
    return (
        run_g * step_g,
        step_g * run_d + run_g * step_d.astype(F32) + prod[:, :N],
        step_g * run_j + step_j.astype(F32) + prod[:, N:],
    )


def kernel(
    q_any,
    k_any,
    v_any,
    decay_any,
    strength_any,
    gate_any,
    gain_any,
    proj_any,
    out_ref,
    q_buf,
    k_buf,
    v_buf,
    decay_buf,
    strength_buf,
    gate_buf,
    gain_buf,
    proj_buf,
    head_send,
    head_recv,
    pre_d,
    pre_j,
    pre_g,
    total_buf,
    state_buf,
    state_send,
    state_recv,
    reach_buf,
    local_buf,
    normed_buf,
    part_buf,
    part_recv,
    load_sem,
    hs_sem,
    hr_sem,
    ts_sem,
    tr_sem,
    ss_sem,
    sr_sem,
    ps_sem,
    pr_sem,
):
    place = lax.axis_index("seq")
    fan = lax.axis_index("head")
    group = place // GROUP
    mine = lax.rem(place, GROUP)
    base = group * GROUP
    chip = lax.rem(mine, ROW) // 2
    owner = lax.rem(mine, 2) == 0
    own_head = chip + 4 * (1 - lax.rem(mine // ROW + chip, 2))
    peers = [lax.rem(mine + step, GROUP) for step in range(1, GROUP)]
    fan_peers = [lax.rem(fan + step, FANS) for step in (2, 1, 3)]

    loads = [
        pltpu.make_async_copy(source, target, load_sem.at[n])
        for n, (source, target) in enumerate(
            (
                (k_any, k_buf),
                (decay_any, decay_buf),
                (strength_any, strength_buf),
                (v_any, v_buf),
                (q_any, q_buf),
                (gate_any, gate_buf),
                (gain_any, gain_buf),
                (proj_any, proj_buf),
            )
        )
    ]
    for load in loads:
        load.start()

    barrier = pltpu.get_barrier_semaphore()
    greeted = [(base + peer, fan) for peer in peers]
    greeted += [(lax.rem(place + step * GROUP, GROUPS * GROUP), fan) for step in range(1, GROUPS)]
    greeted += [(place, peer) for peer in fan_peers]
    for device in greeted:
        pl.semaphore_signal(barrier, inc=1, device_id=device, device_id_type=MESH)

    def remote(source, target, send, recv, device):
        return pltpu.make_async_remote_copy(
            src_ref=source,
            dst_ref=target,
            send_sem=send,
            recv_sem=recv,
            device_id=device,
            device_id_type=MESH,
        )

    def head_copy(h, sender):
        return remote(
            head_send.at[h],
            head_recv.at[sender],
            hs_sem.at[h],
            hr_sem.at[sender],
            (base + OWNERS[h], fan),
        )

    def total_copy(source, target):
        rows = N if source == 0 else MSG
        return remote(
            total_buf.at[source, pl.ds(0, rows)],
            total_buf.at[source, pl.ds(0, rows)],
            ts_sem.at[target],
            tr_sem.at[source],
            (target * GROUP + mine, fan),
        )

    def state_copy(peer):
        return remote(
            state_send.at[peer],
            state_recv.at[own_head],
            ss_sem.at[peer],
            sr_sem.at[own_head],
            (base + peer, fan),
        )

    tri_row = lax.broadcasted_iota(jnp.int32, (N, N), 0)
    tri_col = lax.broadcasted_iota(jnp.int32, (N, N), 1)
    upper = jnp.where(tri_row <= tri_col, 1.0, 0.0).astype(F32)
    for load in loads[1:3]:
        load.wait()
    strength = strength_buf[...]
    cumul = jnp.dot(
        decay_buf[...], upper, precision=lax.Precision.HIGHEST, preferred_element_type=F32
    )
    turned = jnp.concatenate([cumul, strength, jnp.zeros((N - 2 * HEADS, N), F32)], axis=0).T
    loads[0].wait()
    loads[3].wait()
    kept = []
    for start in range(0, HEADS, BATCH):
        heads = range(start, start + BATCH)

        def per_head(buf):
            return jnp.stack([buf[:, h * N : (h + 1) * N] for h in heads])

        cum_row = jnp.stack([cumul[h : h + 1, :] for h in heads])
        str_row = jnp.stack([strength[h : h + 1, :] for h in heads])
        cum_col = jnp.stack([turned[:, h : h + 1] for h in heads])
        str_col = jnp.stack([turned[:, HEADS + h : HEADS + h + 1] for h in heads])
        keyrow = per_head(k_buf)
        ratio, both, ends, last = local_terms(
            keyrow, per_head(v_buf), cum_row, cum_col, str_row, str_col
        )
        kept.append((heads, keyrow, ratio, both, cum_col))
        head_send[start : start + BATCH, N + GROWS :, :] = (-ends[:, :, :N]).astype(BF16)
        head_send[start : start + BATCH, :N, :] = ends[:, :, N:].astype(BF16)
        for n, h in enumerate(heads):
            head_send[h, N : N + GROWS, :] = decay_rows(jnp.broadcast_to(last[n], (GROWS, N)))

        if start == 0:
            pl.semaphore_wait(barrier, len(greeted))
        for h in heads:

            @pl.when(mine != OWNERS[h])
            def _():
                head_copy(h, mine).start()

    loads[4].wait()
    for heads, keyrow, ratio, both, cum_col in kept:
        query = jnp.stack([q_buf[:, h * N : (h + 1) * N] for h in heads])
        reach, local = local_reads(query, keyrow, ratio, both, cum_col)
        reach_buf[heads.start : heads.stop] = reach
        local_buf[heads.start : heads.stop] = local

    @pl.when(owner)
    def _():
        head_recv[mine] = head_send[own_head]
        runs = [None, None]
        for i in range(ROW):
            for n in range(2):
                at = n * ROW + i

                @pl.when(mine != at)
                def _():
                    head_copy(0, at).wait_recv()

                step = read_message(head_recv, at)
                if i == 0:
                    pre_g[at] = jnp.ones((8, N), F32)
                    pre_d[pl.ds(at * N, N), :] = jnp.zeros((N, N), BF16)
                    pre_j[at] = jnp.zeros((N, N), F32)
                    runs[n] = (step[0], step[1].astype(F32), step[2].astype(F32))
                else:
                    run_g, run_d, run_j = runs[n]
                    pre_g[at] = jnp.broadcast_to(run_g, (8, N))
                    pre_d[pl.ds(at * N, N), :] = run_d.astype(BF16)
                    pre_j[at] = run_j
                    runs[n] = advance(runs[n], step)
        (first_g, first_d, first_j), (second_g, second_d, second_j) = runs
        prod = dot_both(second_d, jnp.concatenate([first_d, first_j], axis=1))
        total_buf[group, :N, :] = (second_g * first_j + second_j + prod[:, N:]).astype(BF16)
        total_buf[group, N : N + GROWS, :] = decay_rows(
            jnp.broadcast_to(first_g * second_g, (GROWS, N))
        )
        total_buf[group, N + GROWS :, :] = (
            second_g * first_d + first_g * second_d + prod[:, :N]
        ).astype(BF16)

        for source in range(GROUPS - 1):

            @pl.when(group == source)
            def _():
                for target in range(source + 1, GROUPS):
                    total_copy(source, target).start()

        state_buf[...] = jnp.zeros((N, N), F32)
        for source in range(GROUPS - 1):

            @pl.when(group > source)
            def _():
                total_copy(source, source + 1).wait_recv()
                if source == 0:
                    state_buf[...] = total_buf[0, :N, :].astype(F32)
                else:
                    gain, step_d, step_j = read_message(total_buf, source)
                    state = state_buf[...]
                    state_buf[...] = (
                        gain * state + dot_right(step_d, state) + step_j.astype(F32)
                    )

        state = state_buf[...]
        for n in range(2):
            starts = dot(pre_d[n * ROW * N : (n + 1) * ROW * N, :], state)
            for i in range(ROW):
                at = n * ROW + i
                moved = pre_g[at, :1, :] * state + starts[i * N : (i + 1) * N] + pre_j[at]
                state_send[at] = moved.astype(BF16)
            state = first_g * state + dot_left(first_d, state) + first_j
        for peer in peers:
            state_copy(peer).start()
        state_recv[own_head] = state_send[mine]

    loads[5].wait()
    loads[6].wait()
    gating = jax.nn.sigmoid(gate_buf[...].astype(F32)) * jnp.tile(gain_buf[...], (1, HEADS))
    for h in range(HEADS):

        @pl.when(mine != OWNERS[h])
        def _():
            remote(
                state_send.at[h],
                state_recv.at[h],
                ss_sem.at[h],
                sr_sem.at[h],
                (base + OWNERS[h], fan),
            ).wait_recv()

    outputs = bdot_left(reach_buf[...], state_recv[...]) + local_buf[...]
    square = jnp.mean(outputs * outputs, axis=2, keepdims=True)
    outputs = outputs * lax.rsqrt(square + EPS)
    for h in range(HEADS):
        columns = slice(h * N, (h + 1) * N)
        normed_buf[:, columns] = (outputs[h] * gating[:, columns]).astype(BF16)

    loads[7].wait()
    rows = N // FANS
    width = proj_buf.shape[1] // CHUNKS

    def part_copy(c, n, owner_fan, peer):
        return remote(
            part_buf.at[c, pl.ds(pl.multiple_of(peer * rows, rows), rows), :],
            part_recv.at[c, owner_fan],
            ps_sem.at[c, n],
            pr_sem.at[c, owner_fan],
            (place, peer),
        )

    for c in range(CHUNKS):
        part_buf[c] = jnp.dot(
            normed_buf[...],
            proj_buf[:, c * width : (c + 1) * width],
            preferred_element_type=F32,
        ).astype(BF16)
        for n, peer in enumerate(fan_peers):
            part_copy(c, n, fan, peer).start()
        part_recv[c, fan] = part_buf[c, pl.ds(pl.multiple_of(fan * rows, rows), rows), :]
    for c in range(CHUNKS):
        for n, peer in enumerate(fan_peers):
            part_copy(c, n, peer, peer).wait_recv()
        summed = part_recv[c, 0].astype(F32)
        for n in range(1, FANS):
            summed = summed + part_recv[c, n].astype(F32)
        out_ref[:, c * width : (c + 1) * width] = summed.astype(BF16)

    for h in range(HEADS):

        @pl.when(mine != OWNERS[h])
        def _():
            head_copy(h, mine).wait_send()

    @pl.when(owner)
    def _():
        for source in range(GROUPS - 1):

            @pl.when(group == source)
            def _():
                for target in range(source + 1, GROUPS):
                    total_copy(source, target).wait_send()

        for peer in peers:
            state_copy(peer).wait_send()

    for c in range(CHUNKS):
        for n, peer in enumerate(fan_peers):
            part_copy(c, n, fan, peer).wait_send()


def on_device(
    query_vectors,
    key_vectors,
    value_vectors,
    log_decay,
    write_strength,
    output_gate,
    norm_gain,
    out_proj,
):
    rows, wide = query_vectors.shape
    depth, width = out_proj.shape
    dma = pltpu.SemaphoreType.DMA
    return pl.pallas_call(
        kernel,
        out_shape=jax.ShapeDtypeStruct((rows // FANS, width), BF16),
        in_specs=[pl.BlockSpec(memory_space=pltpu.HBM)] * 8,
        out_specs=pl.BlockSpec(memory_space=pltpu.VMEM),
        scratch_shapes=[
            pltpu.VMEM((rows, wide), BF16),
            pltpu.VMEM((rows, wide), BF16),
            pltpu.VMEM((rows, wide), BF16),
            pltpu.VMEM((HEADS, N), F32),
            pltpu.VMEM((HEADS, N), F32),
            pltpu.VMEM((rows, wide), BF16),
            pltpu.VMEM((1, N), F32),
            pltpu.VMEM((depth, width), BF16),
            pltpu.VMEM((HEADS, MSG, N), BF16),
            pltpu.VMEM((GROUP, MSG, N), BF16),
            pltpu.VMEM((GROUP * N, N), BF16),
            pltpu.VMEM((GROUP, N, N), F32),
            pltpu.VMEM((GROUP, 8, N), F32),
            pltpu.VMEM((GROUPS, MSG, N), BF16),
            pltpu.VMEM((N, N), F32),
            pltpu.VMEM((GROUP, N, N), BF16),
            pltpu.VMEM((HEADS, N, N), BF16),
            pltpu.VMEM((HEADS, N, N), F32),
            pltpu.VMEM((HEADS, N, N), F32),
            pltpu.VMEM((rows, wide), BF16),
            pltpu.VMEM((CHUNKS, rows, width // CHUNKS), BF16),
            pltpu.VMEM((CHUNKS, FANS, rows // FANS, width // CHUNKS), BF16),
            dma((8,)),
            dma((HEADS,)),
            dma((GROUP,)),
            dma((GROUPS,)),
            dma((GROUPS,)),
            dma((GROUP,)),
            dma((HEADS,)),
            dma((CHUNKS, FANS - 1)),
            dma((CHUNKS, FANS)),
        ],
        compiler_params=pltpu.CompilerParams(
            collective_id=0, has_side_effects=True, vmem_limit_bytes=64 * 1024 * 1024
        ),
        cost_estimate=pl.CostEstimate(
            flops=2_000_000_000, bytes_accessed=6_000_000, transcendentals=500_000
        ),
    )(
        query_vectors,
        key_vectors,
        value_vectors,
        log_decay,
        write_strength,
        output_gate,
        norm_gain.reshape(1, N),
        out_proj,
    )


def solution(mesh):
    in_specs = (
        P("seq", "head"),
        P("seq", "head"),
        P("seq", "head"),
        P("head", "seq"),
        P("head", "seq"),
        P("seq", "head"),
        P(),
        P("head", None),
    )
    out_specs = P(("seq", "head"), None)
    return jax.shard_map(
        on_device, mesh=mesh, in_specs=in_specs, out_specs=out_specs, check_vma=False
    )
```

```python
import jax
import jax.numpy as jnp
from jax import lax
from jax.experimental import pallas as pl
from jax.experimental.pallas import tpu as pltpu
from jax.sharding import PartitionSpec as P

MESH = pl.DeviceIdType.MESH
F32 = jnp.float32
BF16 = jnp.bfloat16

ROW = 8
GROUP = 16
GROUPS = 4
QUARTERS = 4
QUARTER = GROUP // QUARTERS
FANS = 4
HEADS = 8
BATCH = 8
N = 128
GROWS = 16
MSG = GROWS + 2 * N
CHUNKS = 3
OWNERS = tuple(ROW * ((h % 4 + h // 4 + 1) % 2) + 2 * (h % 4) for h in range(HEADS))
EPS = 1e-06

FARTHEST = (4, 12, 5, 13, 3, 11, 2, 10, 6, 14, 7, 15, 1, 9, 8)


def bdot(left, right, dims):
    return lax.dot_general(
        left.astype(BF16), right.astype(BF16), (dims, ((0,), (0,))), preferred_element_type=F32
    )


NN = ((2,), (1,))
NT = ((2,), (2,))
TN = ((1,), (1,))


def split(x):
    high = x.astype(BF16)
    return high, (x - high.astype(F32)).astype(BF16)


def bdot_left(left, right):
    return bdot(jnp.concatenate(split(left), axis=2), jnp.concatenate([right, right], axis=1), NN)


def bdot_right_turned(left, right):
    return bdot(
        jnp.concatenate([left, left], axis=1), jnp.concatenate(split(right), axis=1), TN
    )


def bdot_both(left, right):
    lh, ll = split(left)
    rh, rl = split(right)
    return bdot(
        jnp.concatenate([lh, ll, lh], axis=2), jnp.concatenate([rh, rh, rl], axis=1), NN
    )


def dot(left, right):
    return jnp.dot(left.astype(BF16), right.astype(BF16), preferred_element_type=F32)


def dot_turned(left, right):
    return lax.dot_general(
        left.astype(BF16), right.astype(BF16), (((1,), (1,)), ((), ())), preferred_element_type=F32
    )


def thirds(x):
    high = x.astype(BF16)
    rest = x - high.astype(F32)
    middle = rest.astype(BF16)
    return high, middle, (rest - middle.astype(F32)).astype(BF16)


def dot_right(left, right):
    return dot(jnp.concatenate([left, left], axis=1), jnp.concatenate(split(right), axis=0))


def dot_both(left, right):
    lh, ll = split(left)
    rh, rl = split(right)
    return dot(jnp.concatenate([lh, ll, lh], axis=1), jnp.concatenate([rh, rh, rl], axis=0))


def places():
    shape = (1, N, N)
    return lax.broadcasted_iota(jnp.int32, shape, 1), lax.broadcasted_iota(jnp.int32, shape, 2)


def mask(where):
    return jnp.where(where, 1.0, 0.0).astype(F32)


def inverse(couple):
    row, col = places()

    def between(size, count):
        return mask(
            ((row // (count * size)) == (col // (count * size))) & ((row // size) > (col // size))
        )

    eye = mask(row == col)
    solved = eye - couple * between(1, 2)
    size = 2
    while size < N:
        near = solved.astype(BF16)
        step = bdot(near, couple * between(size, 4), NN).astype(BF16)
        prod = bdot(step, jnp.concatenate([step, near], axis=2), NN)
        solved = solved - prod[:, :, N:]
        solved = solved + bdot(prod[:, :, :N], solved, NN)
        size *= 4
    near = solved.astype(BF16)
    solved = near.astype(F32)
    rest = (eye - solved) - bdot_left(couple, near)
    return solved + bdot(near, rest, NN)


def local_solve(keyrow, cum_row, cum_col, str_row, str_col):
    row, col = places()
    keykey = bdot(keyrow, keyrow, NT)
    diag = keykey * mask(row == col)
    kscale_row = lax.rsqrt(jnp.sum(diag, axis=1, keepdims=True) + EPS)
    kscale_col = lax.rsqrt(jnp.sum(diag, axis=2, keepdims=True) + EPS)
    ratio = jnp.exp(jnp.minimum(cum_col - cum_row, 0.0)) * mask(row >= col) * kscale_row
    couple = ratio * keykey * mask(row > col) * (str_col * kscale_col)
    solved = inverse(couple)
    last = cum_row[:, :, N - 1 :]
    return (
        solved * (str_row * jnp.exp(cum_row) * kscale_row),
        solved * str_row,
        ratio,
        jnp.exp(last - cum_col) * kscale_col,
        jnp.exp(last),
    )


def local_ends(keyrow, value, for_key, for_value, tail):
    both = jnp.concatenate([bdot_left(for_key, keyrow), bdot_left(for_value, value)], axis=2)
    return both, bdot_right_turned(keyrow, both * tail)


def local_reads(query, keyrow, ratio, both, cum_col):
    query32 = query.astype(F32)
    qscale = lax.rsqrt(jnp.sum(query32 * query32, axis=2, keepdims=True) + EPS)
    score = ratio * bdot(query, keyrow, NT) * qscale
    read = bdot_both(score, both)
    reach = query32 * (jnp.exp(cum_col) * qscale) - read[:, :, :N]
    return reach, read[:, :, N:]


def decay_rows(gain):
    place = lax.broadcasted_iota(jnp.int32, (GROWS, N), 0)
    high = gain.astype(BF16).astype(F32)
    middle = (gain - high).astype(BF16).astype(F32)
    low = gain - high - middle
    rows = jnp.where(place == 0, high, jnp.where(place == 1, middle, jnp.where(place == 2, low, 0.0)))
    return rows.astype(BF16)


def read_message(buffer, index):
    gain = jnp.sum(buffer[index, N : N + GROWS, :].astype(F32), axis=0, keepdims=True)
    return gain, buffer[index, N + GROWS :, :], buffer[index, :N, :]


def advance(run, step):
    run_g, run_d, run_j = run
    step_g, step_d, step_j = step
    prod = dot_right(step_d, jnp.concatenate([run_d, run_j], axis=1))
    return (
        run_g * step_g,
        step_g * run_d + run_g * step_d.astype(F32) + prod[:, :N],
        step_g * run_j + step_j.astype(F32) + prod[:, N:],
    )


def join(run, step):
    run_g, run_d, run_j = run
    step_g, step_d, step_j = step
    prod = dot_both(step_d, jnp.concatenate([run_d, run_j], axis=1))
    return (
        run_g * step_g,
        step_g * run_d + run_g * step_d + prod[:, :N],
        step_g * run_j + step_j + prod[:, N:],
    )


def kernel(
    q_any,
    k_any,
    v_any,
    decay_any,
    strength_any,
    gate_any,
    gain_any,
    proj_any,
    out_ref,
    q_buf,
    k_buf,
    v_buf,
    decay_buf,
    strength_buf,
    gate_buf,
    gain_buf,
    proj_buf,
    head_send,
    head_recv,
    pre_d,
    pre_j,
    pre_g,
    total_buf,
    state_buf,
    state_send,
    state_recv,
    reach_buf,
    local_buf,
    normed_buf,
    part_buf,
    part_recv,
    load_sem,
    hs_sem,
    hr_sem,
    ts_sem,
    tr_sem,
    ss_sem,
    sr_sem,
    ps_sem,
    pr_sem,
):
    place = lax.axis_index("seq")
    fan = lax.axis_index("head")
    group = place // GROUP
    mine = lax.rem(place, GROUP)
    base = group * GROUP
    chip = lax.rem(mine, ROW) // 2
    owner = lax.rem(mine, 2) == 0
    own_head = chip + 4 * (1 - lax.rem(mine // ROW + chip, 2))
    peers = [lax.rem(mine + step, GROUP) for step in range(1, GROUP)]
    fan_peers = [lax.rem(fan + step, FANS) for step in (2, 1, 3)]

    loads = [
        pltpu.make_async_copy(source, target, load_sem.at[n])
        for n, (source, target) in enumerate(
            (
                (k_any, k_buf),
                (decay_any, decay_buf),
                (strength_any, strength_buf),
                (v_any, v_buf),
                (q_any, q_buf),
                (gate_any, gate_buf),
                (gain_any, gain_buf),
                (proj_any, proj_buf),
            )
        )
    ]
    for load in loads:
        load.start()

    barrier = pltpu.get_barrier_semaphore()
    greeted = [(base + peer, fan) for peer in peers]
    greeted += [(lax.rem(place + step * GROUP, GROUPS * GROUP), fan) for step in range(1, GROUPS)]
    greeted += [(place, peer) for peer in fan_peers]
    for device in greeted:
        pl.semaphore_signal(barrier, inc=1, device_id=device, device_id_type=MESH)

    def remote(source, target, send, recv, device):
        return pltpu.make_async_remote_copy(
            src_ref=source,
            dst_ref=target,
            send_sem=send,
            recv_sem=recv,
            device_id=device,
            device_id_type=MESH,
        )

    def head_copy(h, sender):
        return remote(
            head_send.at[h],
            head_recv.at[sender],
            hs_sem.at[h],
            hr_sem.at[sender],
            (base + OWNERS[h], fan),
        )

    def total_copy(source, target):
        rows = N if source == 0 else MSG
        return remote(
            total_buf.at[source, pl.ds(0, rows)],
            total_buf.at[source, pl.ds(0, rows)],
            ts_sem.at[target],
            tr_sem.at[source],
            (target * GROUP + mine, fan),
        )

    def state_copy(peer):
        return remote(
            state_send.at[peer],
            state_recv.at[own_head],
            ss_sem.at[peer],
            sr_sem.at[own_head],
            (base + peer, fan),
        )

    for load in loads[:4]:
        load.wait()
    row, col = places()
    below = mask(row[0] >= col[0])
    decays, strengths = thirds(decay_buf[...]), thirds(strength_buf[...])
    cumul = sum(dot_turned(third, below) for third in decays)
    cumul_turned = sum(dot_turned(below, third) for third in decays)
    strength = strength_buf[...]
    strength_turned = sum(dot_turned(mask(row[0] == col[0]), third) for third in strengths)
    kept = []
    for start in range(0, HEADS, BATCH):
        heads = range(start, start + BATCH)
        cum_row = jnp.stack([cumul[h : h + 1, :] for h in heads])
        str_row = jnp.stack([strength[h : h + 1, :] for h in heads])
        cum_col = jnp.stack([cumul_turned[:, h : h + 1] for h in heads])
        str_col = jnp.stack([strength_turned[:, h : h + 1] for h in heads])
        keyrow, value = (
            jnp.stack([buf[:, h * N : (h + 1) * N] for h in heads]) for buf in (k_buf, v_buf)
        )
        for_key, for_value, ratio, tail, last = local_solve(
            keyrow, cum_row, cum_col, str_row, str_col
        )
        both, ends = local_ends(keyrow, value, for_key, for_value, tail)
        kept.append((heads, keyrow, ratio, both, cum_col))
        part = slice(start, start + BATCH)
        head_send[part, N + GROWS :, :] = (-ends[:, :, :N]).astype(BF16)
        head_send[part, :N, :] = ends[:, :, N:].astype(BF16)
        for n, h in enumerate(heads):
            head_send[h, N : N + GROWS, :] = decay_rows(jnp.broadcast_to(last[n], (GROWS, N)))

        if start == 0:
            pl.semaphore_wait(barrier, len(greeted))
        for h in heads:

            @pl.when(mine != OWNERS[h])
            def _():
                head_copy(h, mine).start()

    loads[4].wait()
    for heads, keyrow, ratio, both, cum_col in kept:
        query = jnp.stack([q_buf[:, h * N : (h + 1) * N] for h in heads])
        part = slice(heads.start, heads.stop)
        reach_buf[part], local_buf[part] = local_reads(query, keyrow, ratio, both, cum_col)

    @pl.when(owner)
    def _():
        head_recv[mine] = head_send[own_head]
        runs = [None] * QUARTERS
        for i in range(QUARTER):
            for n in range(QUARTERS):
                at = n * QUARTER + i

                @pl.when(mine != at)
                def _():
                    head_copy(0, at).wait_recv()

            for n in range(QUARTERS):
                at = n * QUARTER + i
                step = read_message(head_recv, at)
                if i == 0:
                    pre_g[at] = jnp.ones((8, N), F32)
                    pre_d[pl.ds(at * N, N), :] = jnp.zeros((N, N), BF16)
                    pre_j[at] = jnp.zeros((N, N), F32)
                    runs[n] = (step[0], step[1].astype(F32), step[2].astype(F32))
                else:
                    run_g, run_d, run_j = runs[n]
                    pre_g[at] = jnp.broadcast_to(run_g, (8, N))
                    pre_d[pl.ds(at * N, N), :] = run_d.astype(BF16)
                    pre_j[at] = run_j
                    runs[n] = advance(runs[n], step)
        first_half = join(runs[0], runs[1])
        total_g, total_d, total_j = join(first_half, join(runs[2], runs[3]))
        total_buf[group, :N, :] = total_j.astype(BF16)
        total_buf[group, N : N + GROWS, :] = decay_rows(jnp.broadcast_to(total_g, (GROWS, N)))
        total_buf[group, N + GROWS :, :] = total_d.astype(BF16)

        for source in range(GROUPS - 1):

            @pl.when(group == source)
            def _():
                for target in range(source + 1, GROUPS):
                    total_copy(source, target).start()

        befores = (runs[0], first_half, join(first_half, runs[2]))
        for n, (before_g, before_d, before_j) in enumerate(befores, 1):
            prod = dot_right(
                pre_d[n * QUARTER * N : (n + 1) * QUARTER * N, :],
                jnp.concatenate([before_d, before_j], axis=1),
            )
            for i in range(QUARTER):
                at = n * QUARTER + i
                lines = slice(i * N, (i + 1) * N)
                gain = pre_g[at, :1, :]
                own_d = pre_d[at * N : (at + 1) * N, :].astype(F32)
                pre_j[at] = gain * before_j + pre_j[at] + prod[lines, N:]
                pre_d[at * N : (at + 1) * N, :] = (
                    gain * before_d + before_g * own_d + prod[lines, :N]
                ).astype(BF16)
                pre_g[at] = jnp.broadcast_to(gain * before_g, (8, N))

        state_buf[...] = jnp.zeros((N, N), F32)
        for source in range(GROUPS - 1):

            @pl.when(group > source)
            def _():
                total_copy(source, source + 1).wait_recv()
                if source == 0:
                    state_buf[...] = total_buf[0, :N, :].astype(F32)
                else:
                    gain, step_d, step_j = read_message(total_buf, source)
                    state = state_buf[...]
                    state_buf[...] = (
                        gain * state + dot_right(step_d, state) + step_j.astype(F32)
                    )

        state = state_buf[...]
        for step in FARTHEST + (0,):
            at = lax.rem(mine + step, GROUP)
            moved = dot(pre_d[pl.ds(pl.multiple_of(at * N, N), N), :], state)
            moved = moved + pre_g[at, :1, :] * state + pre_j[at]
            state_send[at] = moved.astype(BF16)
            if step:
                state_copy(at).start()
            else:
                state_recv[own_head] = moved.astype(BF16)

    loads[5].wait()
    loads[6].wait()
    gating = jax.nn.sigmoid(gate_buf[...].astype(F32)) * jnp.tile(gain_buf[...], (1, HEADS))
    for h in range(HEADS):

        @pl.when(mine != OWNERS[h])
        def _():
            remote(
                state_send.at[h],
                state_recv.at[h],
                ss_sem.at[h],
                sr_sem.at[h],
                (base + OWNERS[h], fan),
            ).wait_recv()

    outputs = bdot_left(reach_buf[...], state_recv[...]) + local_buf[...]
    square = jnp.mean(outputs * outputs, axis=2, keepdims=True)
    outputs = outputs * lax.rsqrt(square + EPS)
    for h in range(HEADS):
        columns = slice(h * N, (h + 1) * N)
        normed_buf[:, columns] = (outputs[h] * gating[:, columns]).astype(BF16)

    loads[7].wait()
    rows = N // FANS
    width = proj_buf.shape[1] // CHUNKS

    def part_copy(c, n, owner_fan, peer):
        return remote(
            part_buf.at[c, pl.ds(pl.multiple_of(peer * rows, rows), rows), :],
            part_recv.at[c, owner_fan],
            ps_sem.at[c, n],
            pr_sem.at[c, owner_fan],
            (place, peer),
        )

    for c in range(CHUNKS):
        part_buf[c] = jnp.dot(
            normed_buf[...],
            proj_buf[:, c * width : (c + 1) * width],
            preferred_element_type=F32,
        ).astype(BF16)
        for n, peer in enumerate(fan_peers):
            part_copy(c, n, fan, peer).start()
        part_recv[c, fan] = part_buf[c, pl.ds(pl.multiple_of(fan * rows, rows), rows), :]
    for c in range(CHUNKS):
        for n, peer in enumerate(fan_peers):
            part_copy(c, n, peer, peer).wait_recv()
        summed = part_recv[c, 0].astype(F32)
        for n in range(1, FANS):
            summed = summed + part_recv[c, n].astype(F32)
        out_ref[:, c * width : (c + 1) * width] = summed.astype(BF16)

    for h in range(HEADS):

        @pl.when(mine != OWNERS[h])
        def _():
            head_copy(h, mine).wait_send()

    @pl.when(owner)
    def _():
        for source in range(GROUPS - 1):

            @pl.when(group == source)
            def _():
                for target in range(source + 1, GROUPS):
                    total_copy(source, target).wait_send()

        for peer in peers:
            state_copy(peer).wait_send()

    for c in range(CHUNKS):
        for n, peer in enumerate(fan_peers):
            part_copy(c, n, fan, peer).wait_send()


def on_device(
    query_vectors,
    key_vectors,
    value_vectors,
    log_decay,
    write_strength,
    output_gate,
    norm_gain,
    out_proj,
):
    rows, wide = query_vectors.shape
    depth, width = out_proj.shape
    dma = pltpu.SemaphoreType.DMA
    return pl.pallas_call(
        kernel,
        out_shape=jax.ShapeDtypeStruct((rows // FANS, width), BF16),
        in_specs=[pl.BlockSpec(memory_space=pltpu.HBM)] * 8,
        out_specs=pl.BlockSpec(memory_space=pltpu.VMEM),
        scratch_shapes=[
            pltpu.VMEM((rows, wide), BF16),
            pltpu.VMEM((rows, wide), BF16),
            pltpu.VMEM((rows, wide), BF16),
            pltpu.VMEM((HEADS, N), F32),
            pltpu.VMEM((HEADS, N), F32),
            pltpu.VMEM((rows, wide), BF16),
            pltpu.VMEM((1, N), F32),
            pltpu.VMEM((depth, width), BF16),
            pltpu.VMEM((HEADS, MSG, N), BF16),
            pltpu.VMEM((GROUP, MSG, N), BF16),
            pltpu.VMEM((GROUP * N, N), BF16),
            pltpu.VMEM((GROUP, N, N), F32),
            pltpu.VMEM((GROUP, 8, N), F32),
            pltpu.VMEM((GROUPS, MSG, N), BF16),
            pltpu.VMEM((N, N), F32),
            pltpu.VMEM((GROUP, N, N), BF16),
            pltpu.VMEM((HEADS, N, N), BF16),
            pltpu.VMEM((HEADS, N, N), F32),
            pltpu.VMEM((HEADS, N, N), F32),
            pltpu.VMEM((rows, wide), BF16),
            pltpu.VMEM((CHUNKS, rows, width // CHUNKS), BF16),
            pltpu.VMEM((CHUNKS, FANS, rows // FANS, width // CHUNKS), BF16),
            dma((8,)),
            dma((HEADS,)),
            dma((GROUP,)),
            dma((GROUPS,)),
            dma((GROUPS,)),
            dma((GROUP,)),
            dma((HEADS,)),
            dma((CHUNKS, FANS - 1)),
            dma((CHUNKS, FANS)),
        ],
        compiler_params=pltpu.CompilerParams(
            collective_id=0, has_side_effects=True, vmem_limit_bytes=48 * 1024 * 1024
        ),
        cost_estimate=pl.CostEstimate(
            flops=2_000_000_000, bytes_accessed=6_000_000, transcendentals=500_000
        ),
    )(
        *(
            pltpu.with_memory_space_constraint(array, pltpu.HBM)
            for array in (
                query_vectors,
                key_vectors,
                value_vectors,
                log_decay,
                write_strength,
                output_gate,
                norm_gain.reshape(1, N),
                out_proj,
            )
        )
    )


def solution(mesh):
    in_specs = (
        P("seq", "head"),
        P("seq", "head"),
        P("seq", "head"),
        P("head", "seq"),
        P("head", "seq"),
        P("seq", "head"),
        P(),
        P("head", None),
    )
    out_specs = P(("seq", "head"), None)
    return jax.shard_map(
        on_device, mesh=mesh, in_specs=in_specs, out_specs=out_specs, check_vma=False
    )
```

```python
import jax
import jax.numpy as jnp
from jax import lax
from jax.experimental import pallas as pl
from jax.experimental.pallas import tpu as pltpu
from jax.sharding import PartitionSpec as P

MESH = pl.DeviceIdType.MESH
F32 = jnp.float32
BF16 = jnp.bfloat16

GROUP = 16
GROUPS = 4
CHIPS = GROUP // 2
SIDE = 4
HALVES = 2
HALF = CHIPS // HALVES
FANS = 4
HEADS = 8
SHARE = HEADS // 2
N = 128
GROWS = 16
MSG = GROWS + 2 * N
CHUNKS = 3
EPS = 1e-06
FARTHEST = (2, 6, 1, 3, 5, 7, 4)


def bdot(left, right, dims):
    return lax.dot_general(
        left.astype(BF16), right.astype(BF16), (dims, ((0,), (0,))), preferred_element_type=F32
    )


NN = ((2,), (1,))
NT = ((2,), (2,))
TN = ((1,), (1,))


def split(x):
    high = x.astype(BF16)
    return high, (x - high.astype(F32)).astype(BF16)


def bdot_left(left, right):
    return bdot(jnp.concatenate(split(left), axis=2), jnp.concatenate([right, right], axis=1), NN)


def bdot_right_turned(left, right):
    return bdot(
        jnp.concatenate([left, left], axis=1), jnp.concatenate(split(right), axis=1), TN
    )


def bdot_both(left, right):
    lh, ll = split(left)
    rh, rl = split(right)
    return bdot(
        jnp.concatenate([lh, ll, lh], axis=2), jnp.concatenate([rh, rh, rl], axis=1), NN
    )


def dot(left, right):
    return jnp.dot(left.astype(BF16), right.astype(BF16), preferred_element_type=F32)


def dot_turned(left, right):
    return lax.dot_general(
        left.astype(BF16), right.astype(BF16), (((1,), (1,)), ((), ())), preferred_element_type=F32
    )


def thirds(x):
    high = x.astype(BF16)
    rest = x - high.astype(F32)
    middle = rest.astype(BF16)
    return high, middle, (rest - middle.astype(F32)).astype(BF16)


def dot_right(left, right):
    return dot(jnp.concatenate([left, left], axis=1), jnp.concatenate(split(right), axis=0))


def dot_both(left, right):
    lh, ll = split(left)
    rh, rl = split(right)
    return dot(jnp.concatenate([lh, ll, lh], axis=1), jnp.concatenate([rh, rh, rl], axis=0))


def places():
    shape = (1, N, N)
    return lax.broadcasted_iota(jnp.int32, shape, 1), lax.broadcasted_iota(jnp.int32, shape, 2)


def mask(where):
    return jnp.where(where, 1.0, 0.0).astype(F32)


def inverse(couple):
    row, col = places()

    def between(size, count):
        return mask(
            ((row // (count * size)) == (col // (count * size))) & ((row // size) > (col // size))
        )

    eye = mask(row == col)
    solved = eye - couple * between(1, 2)
    size = 2
    while size < N:
        near = solved.astype(BF16)
        step = bdot(near, couple * between(size, 4), NN).astype(BF16)
        prod = bdot(step, jnp.concatenate([step, near], axis=2), NN)
        solved = solved - prod[:, :, N:]
        solved = solved + bdot(prod[:, :, :N], solved, NN)
        size *= 4
    near = solved.astype(BF16)
    solved = near.astype(F32)
    rest = (eye - solved) - bdot_left(couple, near)
    return solved + bdot(near, rest, NN)


def local_solve(keyrow, cum_row, cum_col, str_row, str_col):
    row, col = places()
    keykey = bdot(keyrow, keyrow, NT)
    diag = keykey * mask(row == col)
    kscale_row = lax.rsqrt(jnp.sum(diag, axis=1, keepdims=True) + EPS)
    kscale_col = lax.rsqrt(jnp.sum(diag, axis=2, keepdims=True) + EPS)
    ratio = jnp.exp(jnp.minimum(cum_col - cum_row, 0.0)) * mask(row >= col) * kscale_row
    couple = ratio * keykey * mask(row > col) * (str_col * kscale_col)
    solved = inverse(couple)
    last = cum_row[:, :, N - 1 :]
    return (
        solved * (str_row * jnp.exp(cum_row) * kscale_row),
        solved * str_row,
        ratio,
        jnp.exp(last - cum_col) * kscale_col,
        jnp.exp(last),
    )


def local_ends(keyrow, value, for_key, for_value, tail):
    both = jnp.concatenate([bdot_left(for_key, keyrow), bdot_left(for_value, value)], axis=2)
    return both, bdot_right_turned(keyrow, both * tail)


def local_reads(query, keyrow, ratio, both, cum_col):
    query32 = query.astype(F32)
    qscale = lax.rsqrt(jnp.sum(query32 * query32, axis=2, keepdims=True) + EPS)
    score = ratio * bdot(query, keyrow, NT) * qscale
    read = bdot_both(score, both)
    reach = query32 * (jnp.exp(cum_col) * qscale) - read[:, :, :N]
    return reach, read[:, :, N:]


def decay_rows(gain):
    place = lax.broadcasted_iota(jnp.int32, gain.shape, gain.ndim - 2)
    high = gain.astype(BF16).astype(F32)
    middle = (gain - high).astype(BF16).astype(F32)
    low = gain - high - middle
    rows = jnp.where(place == 0, high, jnp.where(place == 1, middle, jnp.where(place == 2, low, 0.0)))
    return rows.astype(BF16)


def read_message(message):
    gain = jnp.sum(message[..., N : N + GROWS, :].astype(F32), axis=-2, keepdims=True)
    return gain, message[..., N + GROWS :, :], message[..., :N, :]


def advance(run, step):
    run_g, run_d, run_j = run
    step_g, step_d, step_j = step
    prod = dot_right(step_d, jnp.concatenate([run_d, run_j], axis=1))
    return (
        run_g * step_g,
        step_g * run_d + run_g * step_d.astype(F32) + prod[:, :N],
        step_g * run_j + step_j.astype(F32) + prod[:, N:],
    )


def join(run, step):
    run_g, run_d, run_j = run
    step_g, step_d, step_j = step
    prod = dot_both(step_d, jnp.concatenate([run_d, run_j], axis=1))
    return (
        run_g * step_g,
        step_g * run_d + run_g * step_d + prod[:, :N],
        step_g * run_j + step_j + prod[:, N:],
    )


def kernel(
    q_any,
    k_any,
    v_any,
    decay_any,
    strength_any,
    gate_any,
    gain_any,
    proj_any,
    out_ref,
    q_buf,
    k_buf,
    v_buf,
    decay_buf,
    strength_buf,
    gate_buf,
    gain_buf,
    proj_buf,
    terms,
    chip_send,
    chip_recv,
    pre_d,
    pre_j,
    pre_g,
    total_buf,
    state_buf,
    state_send,
    state_recv,
    reach_buf,
    local_buf,
    normed_buf,
    part_buf,
    part_recv,
    load_sem,
    xs_sem,
    xr_sem,
    cs_sem,
    cr_sem,
    ts_sem,
    tr_sem,
    ss_sem,
    sr_sem,
    ps_sem,
    pr_sem,
):
    place = lax.axis_index("seq")
    fan = lax.axis_index("head")
    group = place // GROUP
    mine = lax.rem(place, GROUP)
    base = group * GROUP
    core = lax.rem(mine, 2)
    chip = mine // 2
    side = lax.rem(chip, SIDE)
    partner = place + 1 - 2 * core
    first_head = core * SHARE
    owner = chip // SIDE == lax.rem(side + core + 1, 2)
    own_head = first_head + side
    peers = [lax.rem(mine + step, GROUP) for step in range(1, GROUP)]
    fan_peers = [lax.rem(fan + step, FANS) for step in (2, 1, 3)]

    loads = [
        pltpu.make_async_copy(source, target, load_sem.at[n])
        for n, (source, target) in enumerate(
            (
                (k_any, k_buf),
                (decay_any, decay_buf),
                (strength_any, strength_buf),
                (v_any, v_buf),
                (q_any, q_buf),
                (gate_any, gate_buf),
                (gain_any, gain_buf),
                (proj_any, proj_buf),
            )
        )
    ]
    for load in loads:
        load.start()

    barrier = pltpu.get_barrier_semaphore()
    greeted = [(base + peer, fan) for peer in peers]
    greeted += [(lax.rem(place + step * GROUP, GROUPS * GROUP), fan) for step in range(1, GROUPS)]
    greeted += [(place, peer) for peer in fan_peers]
    for device in greeted:
        pl.semaphore_signal(barrier, inc=1, device_id=device, device_id_type=MESH)

    def remote(source, target, send, recv, device):
        return pltpu.make_async_remote_copy(
            src_ref=source,
            dst_ref=target,
            send_sem=send,
            recv_sem=recv,
            device_id=device,
            device_id_type=MESH,
        )

    def pair_copy(half, sender):
        part = terms.at[sender, pl.ds(half * SHARE, SHARE)]
        return remote(part, part, xs_sem.at[half], xr_sem.at[half], (partner, fan))

    def owner_chip(n):
        return SIDE * lax.rem(n + core + 1, 2) + n

    def chip_copy(n, sender):
        return remote(
            chip_send.at[n],
            chip_recv.at[sender],
            cs_sem.at[n],
            cr_sem.at[sender],
            (base + 2 * owner_chip(n) + core, fan),
        )

    def total_copy(source, target):
        rows = N if source == 0 else MSG
        return remote(
            total_buf.at[source, pl.ds(0, rows)],
            total_buf.at[source, pl.ds(0, rows)],
            ts_sem.at[target],
            tr_sem.at[source],
            (target * GROUP + mine, fan),
        )

    def state_copy(at):
        return remote(
            state_send.at[at],
            state_recv.at[own_head],
            ss_sem.at[at],
            sr_sem.at[own_head],
            (base + 2 * at + core, fan),
        )

    def share_copy(half):
        part = state_recv.at[pl.ds(half * SHARE, SHARE)]
        return remote(part, part, xs_sem.at[2], xr_sem.at[2], (partner, fan))

    for load in loads[:5]:
        load.wait()
    row, col = places()
    below = mask(row[0] >= col[0])
    decays, strengths = thirds(decay_buf[...]), thirds(strength_buf[...])
    cumul = sum(dot_turned(third, below) for third in decays)
    cumul_turned = sum(dot_turned(below, third) for third in decays)
    strength = strength_buf[...]
    strength_turned = sum(dot_turned(mask(row[0] == col[0]), third) for third in strengths)
    heads = range(HEADS)
    cum_row = jnp.stack([cumul[h : h + 1, :] for h in heads])
    str_row = jnp.stack([strength[h : h + 1, :] for h in heads])
    cum_col = jnp.stack([cumul_turned[:, h : h + 1] for h in heads])
    str_col = jnp.stack([strength_turned[:, h : h + 1] for h in heads])
    query, keyrow, value = (
        jnp.stack([buf[:, h * N : (h + 1) * N] for h in heads]) for buf in (q_buf, k_buf, v_buf)
    )
    for_key, for_value, ratio, tail, last = local_solve(keyrow, cum_row, cum_col, str_row, str_col)
    both, ends = local_ends(keyrow, value, for_key, for_value, tail)
    own = terms.at[core]
    own[:, :N, :] = ends[:, :, N:].astype(BF16)
    own[:, N : N + GROWS, :] = decay_rows(jnp.broadcast_to(last, (HEADS, GROWS, N)))
    own[:, N + GROWS :, :] = (-ends[:, :, :N]).astype(BF16)

    pl.semaphore_wait(barrier, len(greeted))
    pair_copy(1 - core, core).start()

    @pl.when(core == 0)
    def _():
        pair_copy(0, core).start()

    pair_copy(core, 1 - core).wait_recv()
    share = pl.ds(first_head, SHARE)
    first_g, first_d, first_j = read_message(terms[0, share])
    second_g, second_d, second_j = read_message(terms[1, share])
    prod = bdot(second_d, jnp.concatenate([first_d, first_j], axis=2), NN)
    first_d, first_j, second_d, second_j = (
        x.astype(F32) for x in (first_d, first_j, second_d, second_j)
    )
    chip_send[:, :N, :] = (second_g * first_j + second_j + prod[:, :, N:]).astype(BF16)
    chip_send[:, N : N + GROWS, :] = decay_rows(
        jnp.broadcast_to(first_g * second_g, (SHARE, GROWS, N))
    )
    chip_send[:, N + GROWS :, :] = (
        second_g * first_d + first_g * second_d + prod[:, :, :N]
    ).astype(BF16)

    for n in range(SHARE):

        @pl.when(chip != owner_chip(n))
        def _():
            chip_copy(n, chip).start()

    reach, local = local_reads(query, keyrow, ratio, both, cum_col)
    reach_buf[...] = reach
    local_buf[...] = local

    @pl.when(core == 1)
    def _():
        pair_copy(0, 0).wait_recv()
        before_g, before_d, before_j = read_message(terms[0])
        prod = bdot_left(reach_buf[...], jnp.concatenate([before_d, before_j], axis=2))
        reach_buf[...] = before_g * reach_buf[...] + prod[:, :, :N]
        local_buf[...] = local_buf[...] + prod[:, :, N:]

    @pl.when(owner)
    def _():
        chip_recv[chip] = chip_send[side]
        runs = [None] * HALVES
        for i in range(HALF):
            for n in range(HALVES):
                at = n * HALF + i

                @pl.when(chip != at)
                def _():
                    chip_copy(0, at).wait_recv()

            for n in range(HALVES):
                at = n * HALF + i
                step = read_message(chip_recv[at])
                if i == 0:
                    pre_g[at] = jnp.ones((8, N), F32)
                    pre_d[pl.ds(at * N, N), :] = jnp.zeros((N, N), BF16)
                    pre_j[at] = jnp.zeros((N, N), F32)
                    runs[n] = (step[0], step[1].astype(F32), step[2].astype(F32))
                else:
                    run_g, run_d, run_j = runs[n]
                    pre_g[at] = jnp.broadcast_to(run_g, (8, N))
                    pre_d[pl.ds(at * N, N), :] = run_d.astype(BF16)
                    pre_j[at] = run_j
                    runs[n] = advance(runs[n], step)
        total_g, total_d, total_j = join(runs[0], runs[1])
        total_buf[group, :N, :] = total_j.astype(BF16)
        total_buf[group, N : N + GROWS, :] = decay_rows(jnp.broadcast_to(total_g, (GROWS, N)))
        total_buf[group, N + GROWS :, :] = total_d.astype(BF16)

        for source in range(GROUPS - 1):

            @pl.when(group == source)
            def _():
                for target in range(source + 1, GROUPS):
                    total_copy(source, target).start()

        before_g, before_d, before_j = runs[0]
        prod = dot_right(pre_d[HALF * N :, :], jnp.concatenate([before_d, before_j], axis=1))
        for i in range(HALF):
            at = HALF + i
            lines = slice(i * N, (i + 1) * N)
            gain = pre_g[at, :1, :]
            own_d = pre_d[at * N : (at + 1) * N, :].astype(F32)
            pre_j[at] = gain * before_j + pre_j[at] + prod[lines, N:]
            pre_d[at * N : (at + 1) * N, :] = (
                gain * before_d + before_g * own_d + prod[lines, :N]
            ).astype(BF16)
            pre_g[at] = jnp.broadcast_to(gain * before_g, (8, N))

        state_buf[...] = jnp.zeros((N, N), F32)
        for source in range(GROUPS - 1):

            @pl.when(group > source)
            def _():
                total_copy(source, source + 1).wait_recv()
                if source == 0:
                    state_buf[...] = total_buf[0, :N, :].astype(F32)
                else:
                    gain, step_d, step_j = read_message(total_buf[source])
                    state = state_buf[...]
                    state_buf[...] = (
                        gain * state + dot_right(step_d, state) + step_j.astype(F32)
                    )

        state = state_buf[...]
        for step in FARTHEST + (0,):
            at = lax.rem(chip + step, CHIPS)
            moved = dot(pre_d[pl.ds(pl.multiple_of(at * N, N), N), :], state)
            moved = moved + pre_g[at, :1, :] * state + pre_j[at]
            state_send[at] = moved.astype(BF16)
            if step:
                state_copy(at).start()
            else:
                state_recv[own_head] = moved.astype(BF16)

    loads[5].wait()
    loads[6].wait()
    gating = jax.nn.sigmoid(gate_buf[...].astype(F32)) * jnp.tile(gain_buf[...], (1, HEADS))
    for n in range(SHARE):

        @pl.when(chip != owner_chip(n))
        def _():
            head = first_head + n
            remote(
                state_send.at[n],
                state_recv.at[head],
                ss_sem.at[n],
                sr_sem.at[head],
                (base + 2 * owner_chip(n) + core, fan),
            ).wait_recv()

    share_copy(core).start()
    share_copy(1 - core).wait_recv()
    outputs = bdot_left(reach_buf[...], state_recv[...]) + local_buf[...]
    square = jnp.mean(outputs * outputs, axis=2, keepdims=True)
    outputs = outputs * lax.rsqrt(square + EPS)
    for h in range(HEADS):
        columns = slice(h * N, (h + 1) * N)
        normed_buf[:, columns] = (outputs[h] * gating[:, columns]).astype(BF16)

    loads[7].wait()
    rows = N // FANS
    width = proj_buf.shape[1] // CHUNKS

    def part_copy(c, n, owner_fan, peer):
        return remote(
            part_buf.at[c, pl.ds(pl.multiple_of(peer * rows, rows), rows), :],
            part_recv.at[c, owner_fan],
            ps_sem.at[c, n],
            pr_sem.at[c, owner_fan],
            (place, peer),
        )

    for c in range(CHUNKS):
        part_buf[c] = jnp.dot(
            normed_buf[...],
            proj_buf[:, c * width : (c + 1) * width],
            preferred_element_type=F32,
        ).astype(BF16)
        for n, peer in enumerate(fan_peers):
            part_copy(c, n, fan, peer).start()
        part_recv[c, fan] = part_buf[c, pl.ds(pl.multiple_of(fan * rows, rows), rows), :]
    for c in range(CHUNKS):
        for n, peer in enumerate(fan_peers):
            part_copy(c, n, peer, peer).wait_recv()
        summed = part_recv[c, 0].astype(F32)
        for n in range(1, FANS):
            summed = summed + part_recv[c, n].astype(F32)
        out_ref[:, c * width : (c + 1) * width] = summed.astype(BF16)

    pair_copy(1 - core, core).wait_send()

    @pl.when(core == 0)
    def _():
        pair_copy(0, core).wait_send()

    for n in range(SHARE):

        @pl.when(chip != owner_chip(n))
        def _():
            chip_copy(n, chip).wait_send()

    @pl.when(owner)
    def _():
        for source in range(GROUPS - 1):

            @pl.when(group == source)
            def _():
                for target in range(source + 1, GROUPS):
                    total_copy(source, target).wait_send()

        for step in FARTHEST:
            state_copy(lax.rem(chip + step, CHIPS)).wait_send()

    share_copy(core).wait_send()
    for c in range(CHUNKS):
        for n, peer in enumerate(fan_peers):
            part_copy(c, n, fan, peer).wait_send()


def on_device(
    query_vectors,
    key_vectors,
    value_vectors,
    log_decay,
    write_strength,
    output_gate,
    norm_gain,
    out_proj,
):
    rows, wide = query_vectors.shape
    depth, width = out_proj.shape
    dma = pltpu.SemaphoreType.DMA
    return pl.pallas_call(
        kernel,
        out_shape=jax.ShapeDtypeStruct((rows // FANS, width), BF16),
        in_specs=[pl.BlockSpec(memory_space=pltpu.HBM)] * 8,
        out_specs=pl.BlockSpec(memory_space=pltpu.VMEM),
        scratch_shapes=[
            pltpu.VMEM((rows, wide), BF16),
            pltpu.VMEM((rows, wide), BF16),
            pltpu.VMEM((rows, wide), BF16),
            pltpu.VMEM((HEADS, N), F32),
            pltpu.VMEM((HEADS, N), F32),
            pltpu.VMEM((rows, wide), BF16),
            pltpu.VMEM((1, N), F32),
            pltpu.VMEM((depth, width), BF16),
            pltpu.VMEM((2, HEADS, MSG, N), BF16),
            pltpu.VMEM((SHARE, MSG, N), BF16),
            pltpu.VMEM((CHIPS, MSG, N), BF16),
            pltpu.VMEM((CHIPS * N, N), BF16),
            pltpu.VMEM((CHIPS, N, N), F32),
            pltpu.VMEM((CHIPS, 8, N), F32),
            pltpu.VMEM((GROUPS, MSG, N), BF16),
            pltpu.VMEM((N, N), F32),
            pltpu.VMEM((CHIPS, N, N), BF16),
            pltpu.VMEM((HEADS, N, N), BF16),
            pltpu.VMEM((HEADS, N, N), F32),
            pltpu.VMEM((HEADS, N, N), F32),
            pltpu.VMEM((rows, wide), BF16),
            pltpu.VMEM((CHUNKS, rows, width // CHUNKS), BF16),
            pltpu.VMEM((CHUNKS, FANS, rows // FANS, width // CHUNKS), BF16),
            dma((8,)),
            dma((3,)),
            dma((3,)),
            dma((SHARE,)),
            dma((CHIPS,)),
            dma((GROUPS,)),
            dma((GROUPS,)),
            dma((CHIPS,)),
            dma((HEADS,)),
            dma((CHUNKS, FANS - 1)),
            dma((CHUNKS, FANS)),
        ],
        compiler_params=pltpu.CompilerParams(
            collective_id=0, has_side_effects=True, vmem_limit_bytes=48 * 1024 * 1024
        ),
        cost_estimate=pl.CostEstimate(
            flops=2_000_000_000, bytes_accessed=6_000_000, transcendentals=500_000
        ),
    )(
        *(
            pltpu.with_memory_space_constraint(array, pltpu.HBM)
            for array in (
                query_vectors,
                key_vectors,
                value_vectors,
                log_decay,
                write_strength,
                output_gate,
                norm_gain.reshape(1, N),
                out_proj,
            )
        )
    )


def solution(mesh):
    in_specs = (
        P("seq", "head"),
        P("seq", "head"),
        P("seq", "head"),
        P("head", "seq"),
        P("head", "seq"),
        P("seq", "head"),
        P(),
        P("head", None),
    )
    out_specs = P(("seq", "head"), None)
    return jax.shard_map(
        on_device, mesh=mesh, in_specs=in_specs, out_specs=out_specs, check_vma=False
    )
```

```python
import jax
import jax.numpy as jnp
from jax import lax
from jax.experimental import pallas as pl
from jax.experimental.pallas import tpu as pltpu
from jax.sharding import PartitionSpec as P

MESH = pl.DeviceIdType.MESH
F32 = jnp.float32
BF16 = jnp.bfloat16

GROUP = 16
GROUPS = 4
CHIPS = GROUP // 2
SIDE = 4
HALVES = 2
HALF = CHIPS // HALVES
FANS = 4
HEADS = 8
SHARE = HEADS // 2
N = 128
GROWS = 16
MSG = GROWS + 2 * N
CHUNKS = 6
EPS = 1e-06
OWNERS = tuple(
    2 * (SIDE * ((h + h // SHARE + 1) % 2) + h % SHARE) + h // SHARE for h in range(HEADS)
)
FARTHEST = (2, 6, 1, 3, 5, 7, 4)


def bdot(left, right, dims):
    return lax.dot_general(
        left.astype(BF16), right.astype(BF16), (dims, ((0,), (0,))), preferred_element_type=F32
    )


NN = ((2,), (1,))
NT = ((2,), (2,))
TN = ((1,), (1,))


def split(x):
    high = x.astype(BF16)
    return high, (x - high.astype(F32)).astype(BF16)


def bdot_left(left, right):
    return bdot(jnp.concatenate(split(left), axis=2), jnp.concatenate([right, right], axis=1), NN)


def bdot_right_turned(left, right):
    return bdot(
        jnp.concatenate([left, left], axis=1), jnp.concatenate(split(right), axis=1), TN
    )


def bdot_both(left, right):
    lh, ll = split(left)
    rh, rl = split(right)
    return bdot(
        jnp.concatenate([lh, ll, lh], axis=2), jnp.concatenate([rh, rh, rl], axis=1), NN
    )


def dot(left, right):
    return jnp.dot(left.astype(BF16), right.astype(BF16), preferred_element_type=F32)


def dot_turned(left, right):
    return lax.dot_general(
        left.astype(BF16), right.astype(BF16), (((1,), (1,)), ((), ())), preferred_element_type=F32
    )


def thirds(x):
    high = x.astype(BF16)
    rest = x - high.astype(F32)
    middle = rest.astype(BF16)
    return high, middle, (rest - middle.astype(F32)).astype(BF16)


def dot_right(left, right):
    return dot(jnp.concatenate([left, left], axis=1), jnp.concatenate(split(right), axis=0))


def dot_both(left, right):
    lh, ll = split(left)
    rh, rl = split(right)
    return dot(jnp.concatenate([lh, ll, lh], axis=1), jnp.concatenate([rh, rh, rl], axis=0))


def places():
    shape = (1, N, N)
    return lax.broadcasted_iota(jnp.int32, shape, 1), lax.broadcasted_iota(jnp.int32, shape, 2)


def mask(where):
    return jnp.where(where, 1.0, 0.0).astype(F32)


def inverse(couple):
    row, col = places()

    def between(size, count):
        return mask(
            ((row // (count * size)) == (col // (count * size))) & ((row // size) > (col // size))
        )

    eye = mask(row == col)
    solved = eye - couple * between(1, 2)
    size = 2
    while size < N:
        near = solved.astype(BF16)
        step = bdot(near, couple * between(size, 4), NN).astype(BF16)
        prod = bdot(step, jnp.concatenate([step, near], axis=2), NN)
        solved = solved - prod[:, :, N:]
        solved = solved + bdot(prod[:, :, :N], solved, NN)
        size *= 4
    near = solved.astype(BF16)
    solved = near.astype(F32)
    rest = (eye - solved) - bdot_left(couple, near)
    return solved + bdot(near, rest, NN)


def local_solve(keyrow, cum_row, cum_col, str_row, str_col):
    row, col = places()
    keykey = bdot(keyrow, keyrow, NT)
    diag = keykey * mask(row == col)
    kscale_row = lax.rsqrt(jnp.sum(diag, axis=1, keepdims=True) + EPS)
    kscale_col = lax.rsqrt(jnp.sum(diag, axis=2, keepdims=True) + EPS)
    ratio = jnp.exp(jnp.minimum(cum_col - cum_row, 0.0)) * mask(row >= col) * kscale_row
    couple = ratio * keykey * mask(row > col) * (str_col * kscale_col)
    solved = inverse(couple)
    last = cum_row[:, :, N - 1 :]
    return (
        solved * (str_row * jnp.exp(cum_row) * kscale_row),
        solved * str_row,
        ratio,
        jnp.exp(last - cum_col) * kscale_col,
        jnp.exp(last),
    )


def local_ends(keyrow, value, for_key, for_value, tail):
    both = jnp.concatenate([bdot_left(for_key, keyrow), bdot_left(for_value, value)], axis=2)
    return both, bdot_right_turned(keyrow, both * tail)


def local_reads(query, keyrow, ratio, both, cum_col):
    query32 = query.astype(F32)
    qscale = lax.rsqrt(jnp.sum(query32 * query32, axis=2, keepdims=True) + EPS)
    score = ratio * bdot(query, keyrow, NT) * qscale
    read = bdot_both(score, both)
    reach = query32 * (jnp.exp(cum_col) * qscale) - read[:, :, :N]
    return reach, read[:, :, N:]


def decay_rows(gain):
    place = lax.broadcasted_iota(jnp.int32, gain.shape, gain.ndim - 2)
    high = gain.astype(BF16).astype(F32)
    middle = (gain - high).astype(BF16).astype(F32)
    low = gain - high - middle
    rows = jnp.where(place == 0, high, jnp.where(place == 1, middle, jnp.where(place == 2, low, 0.0)))
    return rows.astype(BF16)


def read_message(message):
    gain = jnp.sum(message[..., N : N + GROWS, :].astype(F32), axis=-2, keepdims=True)
    return gain, message[..., N + GROWS :, :], message[..., :N, :]


def advance(run, step):
    run_g, run_d, run_j = run
    step_g, step_d, step_j = step
    prod = dot_right(step_d, jnp.concatenate([run_d, run_j], axis=1))
    return (
        run_g * step_g,
        step_g * run_d + run_g * step_d.astype(F32) + prod[:, :N],
        step_g * run_j + step_j.astype(F32) + prod[:, N:],
    )


def join(run, step):
    run_g, run_d, run_j = run
    step_g, step_d, step_j = step
    prod = dot_both(step_d, jnp.concatenate([run_d, run_j], axis=1))
    return (
        run_g * step_g,
        step_g * run_d + run_g * step_d + prod[:, :N],
        step_g * run_j + step_j + prod[:, N:],
    )


def kernel(
    q_any,
    k_any,
    v_any,
    decay_any,
    strength_any,
    gate_any,
    gain_any,
    proj_any,
    out_ref,
    q_buf,
    k_buf,
    v_buf,
    decay_buf,
    strength_buf,
    gate_buf,
    gain_buf,
    proj_buf,
    terms,
    chip_send,
    chip_recv,
    pre_d,
    pre_j,
    pre_g,
    total_buf,
    state_buf,
    state_send,
    state_recv,
    reach_buf,
    local_buf,
    normed_buf,
    share_buf,
    part_buf,
    sum_buf,
    part_recv,
    load_sem,
    xs_sem,
    xr_sem,
    cs_sem,
    cr_sem,
    ts_sem,
    tr_sem,
    ss_sem,
    sr_sem,
    ps_sem,
    pr_sem,
):
    place = lax.axis_index("seq")
    fan = lax.axis_index("head")
    group = place // GROUP
    mine = lax.rem(place, GROUP)
    base = group * GROUP
    core = lax.rem(mine, 2)
    chip = mine // 2
    side = lax.rem(chip, SIDE)
    partner = place + 1 - 2 * core
    first_head = core * SHARE
    owner = chip // SIDE == lax.rem(side + core + 1, 2)
    own_head = first_head + side
    peers = [lax.rem(mine + step, GROUP) for step in range(1, GROUP)]
    ahead = lax.rem(fan + 1 + 2 * core, FANS)
    behind = lax.rem(fan + 3 - 2 * core, FANS)
    opposite = lax.rem(fan + 2, FANS)

    loads = [
        pltpu.make_async_copy(source, target, load_sem.at[n])
        for n, (source, target) in enumerate(
            (
                (k_any, k_buf),
                (decay_any, decay_buf),
                (strength_any, strength_buf),
                (v_any, v_buf),
                (q_any, q_buf),
                (gate_any, gate_buf),
                (gain_any, gain_buf),
                (proj_any, proj_buf),
            )
        )
    ]
    for load in loads:
        load.start()

    barrier = pltpu.get_barrier_semaphore()
    greeted = [(base + peer, fan) for peer in peers]
    greeted += [(lax.rem(place + step * GROUP, GROUPS * GROUP), fan) for step in range(1, GROUPS)]
    greeted += [(place, ahead), (place, behind)]
    for device in greeted:
        pl.semaphore_signal(barrier, inc=1, device_id=device, device_id_type=MESH)

    def remote(source, target, send, recv, device):
        return pltpu.make_async_remote_copy(
            src_ref=source,
            dst_ref=target,
            send_sem=send,
            recv_sem=recv,
            device_id=device,
            device_id_type=MESH,
        )

    def pair_copy(half, sender):
        part = terms.at[sender, pl.ds(half * SHARE, SHARE)]
        return remote(part, part, xs_sem.at[half], xr_sem.at[half], (partner, fan))

    def owner_chip(n):
        return SIDE * lax.rem(n + core + 1, 2) + n

    def chip_copy(n, sender):
        return remote(
            chip_send.at[n],
            chip_recv.at[sender],
            cs_sem.at[n],
            cr_sem.at[sender],
            (base + 2 * owner_chip(n) + core, fan),
        )

    def total_copy(source, target):
        rows = N if source == 0 else MSG
        return remote(
            total_buf.at[source, pl.ds(0, rows)],
            total_buf.at[source, pl.ds(0, rows)],
            ts_sem.at[target],
            tr_sem.at[source],
            (target * GROUP + mine, fan),
        )

    def state_copy(at, side_core):
        return remote(
            state_send.at[at],
            state_recv.at[own_head],
            ss_sem.at[at, side_core],
            sr_sem.at[own_head],
            (base + 2 * at + side_core, fan),
        )

    def state_copies():
        for step in FARTHEST:
            for side_core in range(2):
                yield state_copy(lax.rem(chip + step, CHIPS), side_core)
        yield state_copy(chip, 1 - core)

    for load in loads[:5]:
        load.wait()
    row, col = places()
    below = mask(row[0] >= col[0])
    decays, strengths = thirds(decay_buf[...]), thirds(strength_buf[...])
    cumul = sum(dot_turned(third, below) for third in decays)
    cumul_turned = sum(dot_turned(below, third) for third in decays)
    strength = strength_buf[...]
    strength_turned = sum(dot_turned(mask(row[0] == col[0]), third) for third in strengths)
    heads = range(HEADS)
    cum_row = jnp.stack([cumul[h : h + 1, :] for h in heads])
    str_row = jnp.stack([strength[h : h + 1, :] for h in heads])
    cum_col = jnp.stack([cumul_turned[:, h : h + 1] for h in heads])
    str_col = jnp.stack([strength_turned[:, h : h + 1] for h in heads])
    query, keyrow, value = (
        jnp.stack([buf[:, h * N : (h + 1) * N] for h in heads]) for buf in (q_buf, k_buf, v_buf)
    )
    for_key, for_value, ratio, tail, last = local_solve(keyrow, cum_row, cum_col, str_row, str_col)
    both, ends = local_ends(keyrow, value, for_key, for_value, tail)
    own = terms.at[core]
    own[:, :N, :] = ends[:, :, N:].astype(BF16)
    own[:, N : N + GROWS, :] = decay_rows(jnp.broadcast_to(last, (HEADS, GROWS, N)))
    own[:, N + GROWS :, :] = (-ends[:, :, :N]).astype(BF16)

    pl.semaphore_wait(barrier, len(greeted))
    pair_copy(1 - core, core).start()

    @pl.when(core == 0)
    def _():
        pair_copy(0, core).start()

    pair_copy(core, 1 - core).wait_recv()
    share = pl.ds(first_head, SHARE)
    first_g, first_d, first_j = read_message(terms[0, share])
    second_g, second_d, second_j = read_message(terms[1, share])
    prod = bdot(second_d, jnp.concatenate([first_d, first_j], axis=2), NN)
    first_d, first_j, second_d, second_j = (
        x.astype(F32) for x in (first_d, first_j, second_d, second_j)
    )
    chip_send[:, :N, :] = (second_g * first_j + second_j + prod[:, :, N:]).astype(BF16)
    chip_send[:, N : N + GROWS, :] = decay_rows(
        jnp.broadcast_to(first_g * second_g, (SHARE, GROWS, N))
    )
    chip_send[:, N + GROWS :, :] = (
        second_g * first_d + first_g * second_d + prod[:, :, :N]
    ).astype(BF16)

    for n in range(SHARE):

        @pl.when(chip != owner_chip(n))
        def _():
            chip_copy(n, chip).start()

    reach, local = local_reads(query, keyrow, ratio, both, cum_col)
    reach_buf[...] = reach
    local_buf[...] = local

    @pl.when(core == 1)
    def _():
        pair_copy(0, 0).wait_recv()
        before_g, before_d, before_j = read_message(terms[0])
        prod = bdot_left(reach_buf[...], jnp.concatenate([before_d, before_j], axis=2))
        reach_buf[...] = before_g * reach_buf[...] + prod[:, :, :N]
        local_buf[...] = local_buf[...] + prod[:, :, N:]

    @pl.when(owner)
    def _():
        chip_recv[chip] = chip_send[side]
        runs = [None] * HALVES
        for i in range(HALF):
            for n in range(HALVES):
                at = n * HALF + i

                @pl.when(chip != at)
                def _():
                    chip_copy(0, at).wait_recv()

            for n in range(HALVES):
                at = n * HALF + i
                step = read_message(chip_recv[at])
                if i == 0:
                    pre_g[at] = jnp.ones((8, N), F32)
                    pre_d[pl.ds(at * N, N), :] = jnp.zeros((N, N), BF16)
                    pre_j[at] = jnp.zeros((N, N), F32)
                    runs[n] = (step[0], step[1].astype(F32), step[2].astype(F32))
                else:
                    run_g, run_d, run_j = runs[n]
                    pre_g[at] = jnp.broadcast_to(run_g, (8, N))
                    pre_d[pl.ds(at * N, N), :] = run_d.astype(BF16)
                    pre_j[at] = run_j
                    runs[n] = advance(runs[n], step)
        total_g, total_d, total_j = join(runs[0], runs[1])
        total_buf[group, :N, :] = total_j.astype(BF16)
        total_buf[group, N : N + GROWS, :] = decay_rows(jnp.broadcast_to(total_g, (GROWS, N)))
        total_buf[group, N + GROWS :, :] = total_d.astype(BF16)

        for source in range(GROUPS - 1):

            @pl.when(group == source)
            def _():
                for target in range(source + 1, GROUPS):
                    total_copy(source, target).start()

        before_g, before_d, before_j = runs[0]
        prod = dot_right(pre_d[HALF * N :, :], jnp.concatenate([before_d, before_j], axis=1))
        for i in range(HALF):
            at = HALF + i
            lines = slice(i * N, (i + 1) * N)
            gain = pre_g[at, :1, :]
            own_d = pre_d[at * N : (at + 1) * N, :].astype(F32)
            pre_j[at] = gain * before_j + pre_j[at] + prod[lines, N:]
            pre_d[at * N : (at + 1) * N, :] = (
                gain * before_d + before_g * own_d + prod[lines, :N]
            ).astype(BF16)
            pre_g[at] = jnp.broadcast_to(gain * before_g, (8, N))

        state_buf[...] = jnp.zeros((N, N), F32)
        for source in range(GROUPS - 1):

            @pl.when(group > source)
            def _():
                total_copy(source, source + 1).wait_recv()
                if source == 0:
                    state_buf[...] = total_buf[0, :N, :].astype(F32)
                else:
                    gain, step_d, step_j = read_message(total_buf[source])
                    state = state_buf[...]
                    state_buf[...] = (
                        gain * state + dot_right(step_d, state) + step_j.astype(F32)
                    )

        state = state_buf[...]
        moved = dot(pre_d[...], state).reshape(CHIPS, N, N) + pre_j[...]
        state_send[...] = (moved + pre_g[:, :1, :] * state).astype(BF16)
        for copy in state_copies():
            copy.start()
        state_recv[own_head] = state_send[chip]

    loads[5].wait()
    loads[6].wait()
    gating = jax.nn.sigmoid(gate_buf[...].astype(F32)) * jnp.tile(gain_buf[...], (1, HEADS))
    for h in range(HEADS):

        @pl.when(mine != OWNERS[h])
        def _():
            remote(
                state_send.at[h],
                state_recv.at[h],
                ss_sem.at[h, 0],
                sr_sem.at[h],
                (base + OWNERS[h], fan),
            ).wait_recv()

    outputs = bdot_left(reach_buf[...], state_recv[...]) + local_buf[...]
    square = jnp.mean(outputs * outputs, axis=2, keepdims=True)
    outputs = outputs * lax.rsqrt(square + EPS)
    for h in range(HEADS):
        columns = slice(h * N, (h + 1) * N)
        normed_buf[:, columns] = (outputs[h] * gating[:, columns]).astype(BF16)

    loads[7].wait()
    rows = N // FANS
    width = proj_buf.shape[1] // CHUNKS

    def lines(owner_fan):
        return pl.ds(pl.multiple_of(owner_fan * rows, rows), rows)

    def part_copy(c, kind):
        source, to = (
            (part_buf.at[c, lines(opposite)], ahead),
            (part_buf.at[c, lines(behind)], behind),
            (sum_buf.at[c], ahead),
        )[kind]
        return remote(
            source, part_recv.at[c, kind], ps_sem.at[c, kind], pr_sem.at[c, kind], (place, to)
        )

    for c in range(CHUNKS):
        share = jnp.dot(
            normed_buf[...],
            proj_buf[:, c * width : (c + 1) * width],
            preferred_element_type=F32,
        )
        part_buf[c] = share.astype(BF16)
        part_copy(c, 0).start()
        share_buf[c] = share
    for c in range(CHUNKS):
        part_copy(c, 1).start()
    for c in range(CHUNKS):
        part_copy(c, 0).wait_recv()
        summed = share_buf[c, lines(ahead)] + part_recv[c, 0].astype(F32)
        sum_buf[c] = summed.astype(BF16)
        part_copy(c, 2).start()
    for c in range(CHUNKS):
        part_copy(c, 1).wait_recv()
        part_copy(c, 2).wait_recv()
        summed = share_buf[c, lines(fan)] + part_recv[c, 1].astype(F32)
        summed = summed + part_recv[c, 2].astype(F32)
        out_ref[:, c * width : (c + 1) * width] = summed.astype(BF16)

    pair_copy(1 - core, core).wait_send()

    @pl.when(core == 0)
    def _():
        pair_copy(0, core).wait_send()

    for n in range(SHARE):

        @pl.when(chip != owner_chip(n))
        def _():
            chip_copy(n, chip).wait_send()

    @pl.when(owner)
    def _():
        for source in range(GROUPS - 1):

            @pl.when(group == source)
            def _():
                for target in range(source + 1, GROUPS):
                    total_copy(source, target).wait_send()

        for copy in state_copies():
            copy.wait_send()

    for c in range(CHUNKS):
        for kind in range(3):
            part_copy(c, kind).wait_send()


def on_device(
    query_vectors,
    key_vectors,
    value_vectors,
    log_decay,
    write_strength,
    output_gate,
    norm_gain,
    out_proj,
):
    rows, wide = query_vectors.shape
    depth, width = out_proj.shape
    dma = pltpu.SemaphoreType.DMA
    return pl.pallas_call(
        kernel,
        out_shape=jax.ShapeDtypeStruct((rows // FANS, width), BF16),
        in_specs=[pl.BlockSpec(memory_space=pltpu.HBM)] * 8,
        out_specs=pl.BlockSpec(memory_space=pltpu.VMEM),
        scratch_shapes=[
            pltpu.VMEM((rows, wide), BF16),
            pltpu.VMEM((rows, wide), BF16),
            pltpu.VMEM((rows, wide), BF16),
            pltpu.VMEM((HEADS, N), F32),
            pltpu.VMEM((HEADS, N), F32),
            pltpu.VMEM((rows, wide), BF16),
            pltpu.VMEM((1, N), F32),
            pltpu.VMEM((depth, width), BF16),
            pltpu.VMEM((2, HEADS, MSG, N), BF16),
            pltpu.VMEM((SHARE, MSG, N), BF16),
            pltpu.VMEM((CHIPS, MSG, N), BF16),
            pltpu.VMEM((CHIPS * N, N), BF16),
            pltpu.VMEM((CHIPS, N, N), F32),
            pltpu.VMEM((CHIPS, 8, N), F32),
            pltpu.VMEM((GROUPS, MSG, N), BF16),
            pltpu.VMEM((N, N), F32),
            pltpu.VMEM((CHIPS, N, N), BF16),
            pltpu.VMEM((HEADS, N, N), BF16),
            pltpu.VMEM((HEADS, N, N), F32),
            pltpu.VMEM((HEADS, N, N), F32),
            pltpu.VMEM((rows, wide), BF16),
            pltpu.VMEM((CHUNKS, rows, width // CHUNKS), F32),
            pltpu.VMEM((CHUNKS, rows, width // CHUNKS), BF16),
            pltpu.VMEM((CHUNKS, rows // FANS, width // CHUNKS), BF16),
            pltpu.VMEM((CHUNKS, 3, rows // FANS, width // CHUNKS), BF16),
            dma((8,)),
            dma((2,)),
            dma((2,)),
            dma((SHARE,)),
            dma((CHIPS,)),
            dma((GROUPS,)),
            dma((GROUPS,)),
            dma((CHIPS, 2)),
            dma((HEADS,)),
            dma((CHUNKS, 3)),
            dma((CHUNKS, 3)),
        ],
        compiler_params=pltpu.CompilerParams(
            collective_id=0, has_side_effects=True, vmem_limit_bytes=48 * 1024 * 1024
        ),
        cost_estimate=pl.CostEstimate(
            flops=2_000_000_000, bytes_accessed=6_000_000, transcendentals=500_000
        ),
    )(
        *(
            pltpu.with_memory_space_constraint(array, pltpu.HBM)
            for array in (
                query_vectors,
                key_vectors,
                value_vectors,
                log_decay,
                write_strength,
                output_gate,
                norm_gain.reshape(1, N),
                out_proj,
            )
        )
    )


def solution(mesh):
    in_specs = (
        P("seq", "head"),
        P("seq", "head"),
        P("seq", "head"),
        P("head", "seq"),
        P("head", "seq"),
        P("seq", "head"),
        P(),
        P("head", None),
    )
    out_specs = P(("seq", "head"), None)
    return jax.shard_map(
        on_device, mesh=mesh, in_specs=in_specs, out_specs=out_specs, check_vma=False
    )
```

```python
import jax
import jax.numpy as jnp
from jax import lax
from jax.experimental import pallas as pl
from jax.experimental.pallas import tpu as pltpu
from jax.sharding import PartitionSpec as P

MESH = pl.DeviceIdType.MESH
F32 = jnp.float32
BF16 = jnp.bfloat16

GROUP = 16
GROUPS = 4
CHIPS = GROUP // 2
SIDE = 4
HALVES = 2
HALF = CHIPS // HALVES
FANS = 4
HEADS = 8
SHARE = HEADS // 2
N = 128
GROWS = 16
MSG = GROWS + 2 * N
CHUNKS = 6
EPS = 1e-06
OWNERS = tuple(
    2 * (SIDE * ((h + h // SHARE + 1) % 2) + h % SHARE) + h // SHARE for h in range(HEADS)
)
FARTHEST = (2, 6, 1, 3, 5, 7, 4)


def bdot(left, right, dims):
    return lax.dot_general(
        left.astype(BF16), right.astype(BF16), (dims, ((0,), (0,))), preferred_element_type=F32
    )


NN = ((2,), (1,))
NT = ((2,), (2,))
TN = ((1,), (1,))


def split(x):
    high = x.astype(BF16)
    return high, (x - high.astype(F32)).astype(BF16)


def bdot_left(left, right):
    return bdot(jnp.concatenate(split(left), axis=2), jnp.concatenate([right, right], axis=1), NN)


def bdot_right_turned(left, right):
    return bdot(
        jnp.concatenate([left, left], axis=1), jnp.concatenate(split(right), axis=1), TN
    )


def bdot_both(left, right):
    lh, ll = split(left)
    rh, rl = split(right)
    return bdot(
        jnp.concatenate([lh, ll, lh], axis=2), jnp.concatenate([rh, rh, rl], axis=1), NN
    )


def dot(left, right):
    return jnp.dot(left.astype(BF16), right.astype(BF16), preferred_element_type=F32)


def dot_turned(left, right):
    return lax.dot_general(
        left.astype(BF16), right.astype(BF16), (((1,), (1,)), ((), ())), preferred_element_type=F32
    )


def thirds(x):
    high = x.astype(BF16)
    rest = x - high.astype(F32)
    middle = rest.astype(BF16)
    return high, middle, (rest - middle.astype(F32)).astype(BF16)


def dot_right(left, right):
    return dot(jnp.concatenate([left, left], axis=1), jnp.concatenate(split(right), axis=0))


def dot_both(left, right):
    lh, ll = split(left)
    rh, rl = split(right)
    return dot(jnp.concatenate([lh, ll, lh], axis=1), jnp.concatenate([rh, rh, rl], axis=0))


def places():
    shape = (1, N, N)
    return lax.broadcasted_iota(jnp.int32, shape, 1), lax.broadcasted_iota(jnp.int32, shape, 2)


def mask(where):
    return jnp.where(where, 1.0, 0.0).astype(F32)


def inverse(couple):
    row, col = places()

    def between(size, count):
        return mask(
            ((row // (count * size)) == (col // (count * size))) & ((row // size) > (col // size))
        )

    eye = mask(row == col)
    solved = eye - couple * between(1, 2)
    size = 2
    while size < N:
        near = solved.astype(BF16)
        step = bdot(near, couple * between(size, 4), NN).astype(BF16)
        prod = bdot(step, jnp.concatenate([step, near], axis=2), NN)
        solved = solved - prod[:, :, N:]
        solved = solved + bdot(prod[:, :, :N], solved, NN)
        size *= 4
    near = solved.astype(BF16)
    solved = near.astype(F32)
    rest = (eye - solved) - bdot_left(couple, near)
    return solved + bdot(near, rest, NN)


def local_solve(keyrow, cum_row, cum_col, str_row, str_col):
    row, col = places()
    keykey = bdot(keyrow, keyrow, NT)
    diag = keykey * mask(row == col)
    kscale_row = lax.rsqrt(jnp.sum(diag, axis=1, keepdims=True) + EPS)
    kscale_col = lax.rsqrt(jnp.sum(diag, axis=2, keepdims=True) + EPS)
    ratio = jnp.exp(jnp.minimum(cum_col - cum_row, 0.0)) * mask(row >= col) * kscale_row
    couple = ratio * keykey * mask(row > col) * (str_col * kscale_col)
    solved = inverse(couple)
    last = cum_row[:, :, N - 1 :]
    return (
        solved * (str_row * jnp.exp(cum_row) * kscale_row),
        solved * str_row,
        ratio,
        jnp.exp(last - cum_col) * kscale_col,
        jnp.exp(last),
    )


def local_ends(keyrow, value, for_key, for_value, tail):
    both = jnp.concatenate([bdot_left(for_key, keyrow), bdot_left(for_value, value)], axis=2)
    return both, bdot_right_turned(keyrow, both * tail)


def local_reads(query, keyrow, ratio, both, cum_col):
    query32 = query.astype(F32)
    qscale = lax.rsqrt(jnp.sum(query32 * query32, axis=2, keepdims=True) + EPS)
    score = ratio * bdot(query, keyrow, NT) * qscale
    read = bdot_both(score, both)
    reach = query32 * (jnp.exp(cum_col) * qscale) - read[:, :, :N]
    return reach, read[:, :, N:]


def decay_rows(gain):
    place = lax.broadcasted_iota(jnp.int32, gain.shape, gain.ndim - 2)
    high = gain.astype(BF16).astype(F32)
    middle = (gain - high).astype(BF16).astype(F32)
    low = gain - high - middle
    rows = jnp.where(place == 0, high, jnp.where(place == 1, middle, jnp.where(place == 2, low, 0.0)))
    return rows.astype(BF16)


def read_message(message):
    gain = jnp.sum(message[..., N : N + GROWS, :].astype(F32), axis=-2, keepdims=True)
    return gain, message[..., N + GROWS :, :], message[..., :N, :]


def advance(run, step):
    run_g, run_d, run_j = run
    step_g, step_d, step_j = step
    prod = dot_right(step_d, jnp.concatenate([run_d, run_j], axis=1))
    return (
        run_g * step_g,
        step_g * run_d + run_g * step_d.astype(F32) + prod[:, :N],
        step_g * run_j + step_j.astype(F32) + prod[:, N:],
    )


def join(run, step):
    run_g, run_d, run_j = run
    step_g, step_d, step_j = step
    prod = dot_both(step_d, jnp.concatenate([run_d, run_j], axis=1))
    return (
        run_g * step_g,
        step_g * run_d + run_g * step_d + prod[:, :N],
        step_g * run_j + step_j + prod[:, N:],
    )


def kernel(
    q_any,
    k_any,
    v_any,
    decay_any,
    strength_any,
    gate_any,
    gain_any,
    proj_any,
    out_ref,
    q_buf,
    k_buf,
    v_buf,
    decay_buf,
    strength_buf,
    gate_buf,
    gain_buf,
    proj_buf,
    terms,
    chip_send,
    chip_recv,
    pre_d,
    pre_j,
    pre_g,
    total_buf,
    state_buf,
    state_send,
    state_recv,
    reach_buf,
    local_buf,
    normed_buf,
    share_buf,
    part_buf,
    sum_buf,
    part_recv,
    load_sem,
    xs_sem,
    xr_sem,
    cs_sem,
    cr_sem,
    ts_sem,
    tr_sem,
    ss_sem,
    sr_sem,
    ps_sem,
    pr_sem,
):
    place = lax.axis_index("seq")
    fan = lax.axis_index("head")
    group = place // GROUP
    mine = lax.rem(place, GROUP)
    base = group * GROUP
    core = lax.rem(mine, 2)
    chip = mine // 2
    side = lax.rem(chip, SIDE)
    partner = place + 1 - 2 * core
    first_head = core * SHARE
    owner = chip // SIDE == lax.rem(side + core + 1, 2)
    own_head = first_head + side
    peers = [lax.rem(mine + step, GROUP) for step in range(1, GROUP)]
    ahead = lax.rem(fan + 1 + 2 * core, FANS)
    behind = lax.rem(fan + 3 - 2 * core, FANS)
    opposite = lax.rem(fan + 2, FANS)

    loads = [
        pltpu.make_async_copy(source, target, load_sem.at[n])
        for n, (source, target) in enumerate(
            (
                (decay_any, decay_buf),
                (strength_any, strength_buf),
                (k_any, k_buf),
                (v_any, v_buf),
                (q_any, q_buf),
                (gate_any, gate_buf),
                (gain_any, gain_buf),
                (proj_any, proj_buf),
            )
        )
    ]
    for load in loads:
        load.start()

    barrier = pltpu.get_barrier_semaphore()
    greeted = [(base + peer, fan) for peer in peers]
    greeted += [(lax.rem(place + step * GROUP, GROUPS * GROUP), fan) for step in range(1, GROUPS)]
    greeted += [(place, ahead), (place, behind)]
    for device in greeted:
        pl.semaphore_signal(barrier, inc=1, device_id=device, device_id_type=MESH)

    def remote(source, target, send, recv, device):
        return pltpu.make_async_remote_copy(
            src_ref=source,
            dst_ref=target,
            send_sem=send,
            recv_sem=recv,
            device_id=device,
            device_id_type=MESH,
        )

    def pair_copy(half, sender):
        part = terms.at[sender, pl.ds(half * SHARE, SHARE)]
        return remote(part, part, xs_sem.at[half], xr_sem.at[half], (partner, fan))

    def owner_chip(n):
        return SIDE * lax.rem(n + core + 1, 2) + n

    def chip_copy(n, sender):
        return remote(
            chip_send.at[n],
            chip_recv.at[sender],
            cs_sem.at[n],
            cr_sem.at[sender],
            (base + 2 * owner_chip(n) + core, fan),
        )

    def total_copy(source, target):
        rows = N if source == 0 else MSG
        return remote(
            total_buf.at[source, pl.ds(0, rows)],
            total_buf.at[source, pl.ds(0, rows)],
            ts_sem.at[target],
            tr_sem.at[source],
            (target * GROUP + mine, fan),
        )

    def state_copy(at, side_core):
        return remote(
            state_send.at[at],
            state_recv.at[own_head],
            ss_sem.at[at, side_core],
            sr_sem.at[own_head],
            (base + 2 * at + side_core, fan),
        )

    def state_copies():
        for step in FARTHEST:
            for side_core in range(2):
                yield state_copy(lax.rem(chip + step, CHIPS), side_core)
        yield state_copy(chip, 1 - core)

    for load in loads[:3]:
        load.wait()
    row, col = places()
    below = mask(row[0] >= col[0])
    decays, strengths = thirds(decay_buf[...]), thirds(strength_buf[...])
    cumul = sum(dot_turned(third, below) for third in decays)
    cumul_turned = sum(dot_turned(below, third) for third in decays)
    strength = strength_buf[...]
    strength_turned = sum(dot_turned(mask(row[0] == col[0]), third) for third in strengths)
    heads = range(HEADS)
    cum_row = jnp.stack([cumul[h : h + 1, :] for h in heads])
    str_row = jnp.stack([strength[h : h + 1, :] for h in heads])
    cum_col = jnp.stack([cumul_turned[:, h : h + 1] for h in heads])
    str_col = jnp.stack([strength_turned[:, h : h + 1] for h in heads])

    def per_head(buf):
        return jnp.stack([buf[:, h * N : (h + 1) * N] for h in heads])

    keyrow = per_head(k_buf)
    for_key, for_value, ratio, tail, last = local_solve(keyrow, cum_row, cum_col, str_row, str_col)
    loads[3].wait()
    both, ends = local_ends(keyrow, per_head(v_buf), for_key, for_value, tail)
    own = terms.at[core]
    own[:, :N, :] = ends[:, :, N:].astype(BF16)
    own[:, N : N + GROWS, :] = decay_rows(jnp.broadcast_to(last, (HEADS, GROWS, N)))
    own[:, N + GROWS :, :] = (-ends[:, :, :N]).astype(BF16)

    pl.semaphore_wait(barrier, len(greeted))
    pair_copy(1 - core, core).start()

    @pl.when(core == 0)
    def _():
        pair_copy(0, core).start()

    pair_copy(core, 1 - core).wait_recv()
    share = pl.ds(first_head, SHARE)
    first_g, first_d, first_j = read_message(terms[0, share])
    second_g, second_d, second_j = read_message(terms[1, share])
    prod = bdot(second_d, jnp.concatenate([first_d, first_j], axis=2), NN)
    first_d, first_j, second_d, second_j = (
        x.astype(F32) for x in (first_d, first_j, second_d, second_j)
    )
    chip_send[:, :N, :] = (second_g * first_j + second_j + prod[:, :, N:]).astype(BF16)
    chip_send[:, N : N + GROWS, :] = decay_rows(
        jnp.broadcast_to(first_g * second_g, (SHARE, GROWS, N))
    )
    chip_send[:, N + GROWS :, :] = (
        second_g * first_d + first_g * second_d + prod[:, :, :N]
    ).astype(BF16)

    for n in range(SHARE):

        @pl.when(chip != owner_chip(n))
        def _():
            chip_copy(n, chip).start()

    loads[4].wait()
    reach, local = local_reads(per_head(q_buf), keyrow, ratio, both, cum_col)
    reach_buf[...] = reach
    local_buf[...] = local

    @pl.when(core == 1)
    def _():
        pair_copy(0, 0).wait_recv()
        before_g, before_d, before_j = read_message(terms[0])
        prod = bdot_left(reach_buf[...], jnp.concatenate([before_d, before_j], axis=2))
        reach_buf[...] = before_g * reach_buf[...] + prod[:, :, :N]
        local_buf[...] = local_buf[...] + prod[:, :, N:]

    @pl.when(owner)
    def _():
        chip_recv[chip] = chip_send[side]
        runs = [None] * HALVES
        for i in range(HALF):
            for n in range(HALVES):
                at = n * HALF + i

                @pl.when(chip != at)
                def _():
                    chip_copy(0, at).wait_recv()

            for n in range(HALVES):
                at = n * HALF + i
                step = read_message(chip_recv[at])
                if i == 0:
                    pre_g[at] = jnp.ones((8, N), F32)
                    pre_d[pl.ds(at * N, N), :] = jnp.zeros((N, N), BF16)
                    pre_j[at] = jnp.zeros((N, N), F32)
                    runs[n] = (step[0], step[1].astype(F32), step[2].astype(F32))
                else:
                    run_g, run_d, run_j = runs[n]
                    pre_g[at] = jnp.broadcast_to(run_g, (8, N))
                    pre_d[pl.ds(at * N, N), :] = run_d.astype(BF16)
                    pre_j[at] = run_j
                    runs[n] = advance(runs[n], step)
        total_g, total_d, total_j = join(runs[0], runs[1])
        total_buf[group, :N, :] = total_j.astype(BF16)
        total_buf[group, N : N + GROWS, :] = decay_rows(jnp.broadcast_to(total_g, (GROWS, N)))
        total_buf[group, N + GROWS :, :] = total_d.astype(BF16)

        for source in range(GROUPS - 1):

            @pl.when(group == source)
            def _():
                for target in reversed(range(source + 1, GROUPS)):
                    total_copy(source, target).start()

        before_g, before_d, before_j = runs[0]
        prod = dot_right(pre_d[HALF * N :, :], jnp.concatenate([before_d, before_j], axis=1))
        for i in range(HALF):
            at = HALF + i
            lines = slice(i * N, (i + 1) * N)
            gain = pre_g[at, :1, :]
            own_d = pre_d[at * N : (at + 1) * N, :].astype(F32)
            pre_j[at] = gain * before_j + pre_j[at] + prod[lines, N:]
            pre_d[at * N : (at + 1) * N, :] = (
                gain * before_d + before_g * own_d + prod[lines, :N]
            ).astype(BF16)
            pre_g[at] = jnp.broadcast_to(gain * before_g, (8, N))

        state_buf[...] = jnp.zeros((N, N), F32)
        for source in range(GROUPS - 1):

            @pl.when(group > source)
            def _():
                total_copy(source, source + 1).wait_recv()
                if source == 0:
                    state_buf[...] = total_buf[0, :N, :].astype(F32)
                else:
                    gain, step_d, step_j = read_message(total_buf[source])
                    state = state_buf[...]
                    state_buf[...] = (
                        gain * state + dot_right(step_d, state) + step_j.astype(F32)
                    )

        state = state_buf[...]
        moved = dot(pre_d[...], state).reshape(CHIPS, N, N) + pre_j[...]
        state_send[...] = (moved + pre_g[:, :1, :] * state).astype(BF16)
        for copy in state_copies():
            copy.start()
        state_recv[own_head] = state_send[chip]

    loads[5].wait()
    loads[6].wait()
    gating = jax.nn.sigmoid(gate_buf[...].astype(F32)) * jnp.tile(gain_buf[...], (1, HEADS))
    for h in range(HEADS):

        @pl.when(mine != OWNERS[h])
        def _():
            remote(
                state_send.at[h],
                state_recv.at[h],
                ss_sem.at[h, 0],
                sr_sem.at[h],
                (base + OWNERS[h], fan),
            ).wait_recv()

    outputs = bdot_left(reach_buf[...], state_recv[...]) + local_buf[...]
    square = jnp.mean(outputs * outputs, axis=2, keepdims=True)
    outputs = outputs * lax.rsqrt(square + EPS)
    for h in range(HEADS):
        columns = slice(h * N, (h + 1) * N)
        normed_buf[:, columns] = (outputs[h] * gating[:, columns]).astype(BF16)

    loads[7].wait()
    rows = N // FANS
    width = proj_buf.shape[1] // CHUNKS

    def lines(owner_fan):
        return pl.ds(pl.multiple_of(owner_fan * rows, rows), rows)

    def part_copy(c, kind):
        source, to = (
            (part_buf.at[c, lines(opposite)], ahead),
            (part_buf.at[c, lines(behind)], behind),
            (sum_buf.at[c], ahead),
        )[kind]
        return remote(
            source, part_recv.at[c, kind], ps_sem.at[c, kind], pr_sem.at[c, kind], (place, to)
        )

    for c in range(CHUNKS):
        share = jnp.dot(
            normed_buf[...],
            proj_buf[:, c * width : (c + 1) * width],
            preferred_element_type=F32,
        )
        part_buf[c] = share.astype(BF16)
        part_copy(c, 0).start()
        share_buf[c] = share
    for c in range(CHUNKS):
        part_copy(c, 1).start()
    for c in range(CHUNKS):
        part_copy(c, 0).wait_recv()
        summed = share_buf[c, lines(ahead)] + part_recv[c, 0].astype(F32)
        sum_buf[c] = summed.astype(BF16)
        part_copy(c, 2).start()
    for c in range(CHUNKS):
        part_copy(c, 1).wait_recv()
        part_copy(c, 2).wait_recv()
        summed = share_buf[c, lines(fan)] + part_recv[c, 1].astype(F32)
        summed = summed + part_recv[c, 2].astype(F32)
        out_ref[:, c * width : (c + 1) * width] = summed.astype(BF16)

    pair_copy(1 - core, core).wait_send()

    @pl.when(core == 0)
    def _():
        pair_copy(0, core).wait_send()

    for n in range(SHARE):

        @pl.when(chip != owner_chip(n))
        def _():
            chip_copy(n, chip).wait_send()

    @pl.when(owner)
    def _():
        for source in range(GROUPS - 1):

            @pl.when(group == source)
            def _():
                for target in range(source + 1, GROUPS):
                    total_copy(source, target).wait_send()

        for copy in state_copies():
            copy.wait_send()

    for c in range(CHUNKS):
        for kind in range(3):
            part_copy(c, kind).wait_send()


def on_device(
    query_vectors,
    key_vectors,
    value_vectors,
    log_decay,
    write_strength,
    output_gate,
    norm_gain,
    out_proj,
):
    rows, wide = query_vectors.shape
    depth, width = out_proj.shape
    dma = pltpu.SemaphoreType.DMA
    return pl.pallas_call(
        kernel,
        out_shape=jax.ShapeDtypeStruct((rows // FANS, width), BF16),
        in_specs=[pl.BlockSpec(memory_space=pltpu.HBM)] * 8,
        out_specs=pl.BlockSpec(memory_space=pltpu.VMEM),
        scratch_shapes=[
            pltpu.VMEM((rows, wide), BF16),
            pltpu.VMEM((rows, wide), BF16),
            pltpu.VMEM((rows, wide), BF16),
            pltpu.VMEM((HEADS, N), F32),
            pltpu.VMEM((HEADS, N), F32),
            pltpu.VMEM((rows, wide), BF16),
            pltpu.VMEM((1, N), F32),
            pltpu.VMEM((depth, width), BF16),
            pltpu.VMEM((2, HEADS, MSG, N), BF16),
            pltpu.VMEM((SHARE, MSG, N), BF16),
            pltpu.VMEM((CHIPS, MSG, N), BF16),
            pltpu.VMEM((CHIPS * N, N), BF16),
            pltpu.VMEM((CHIPS, N, N), F32),
            pltpu.VMEM((CHIPS, 8, N), F32),
            pltpu.VMEM((GROUPS, MSG, N), BF16),
            pltpu.VMEM((N, N), F32),
            pltpu.VMEM((CHIPS, N, N), BF16),
            pltpu.VMEM((HEADS, N, N), BF16),
            pltpu.VMEM((HEADS, N, N), F32),
            pltpu.VMEM((HEADS, N, N), F32),
            pltpu.VMEM((rows, wide), BF16),
            pltpu.VMEM((CHUNKS, rows, width // CHUNKS), F32),
            pltpu.VMEM((CHUNKS, rows, width // CHUNKS), BF16),
            pltpu.VMEM((CHUNKS, rows // FANS, width // CHUNKS), BF16),
            pltpu.VMEM((CHUNKS, 3, rows // FANS, width // CHUNKS), BF16),
            dma((8,)),
            dma((2,)),
            dma((2,)),
            dma((SHARE,)),
            dma((CHIPS,)),
            dma((GROUPS,)),
            dma((GROUPS,)),
            dma((CHIPS, 2)),
            dma((HEADS,)),
            dma((CHUNKS, 3)),
            dma((CHUNKS, 3)),
        ],
        compiler_params=pltpu.CompilerParams(
            collective_id=0, has_side_effects=True, vmem_limit_bytes=48 * 1024 * 1024
        ),
        cost_estimate=pl.CostEstimate(
            flops=2_000_000_000, bytes_accessed=6_000_000, transcendentals=500_000
        ),
    )(
        *(
            pltpu.with_memory_space_constraint(array, pltpu.HBM)
            for array in (
                query_vectors,
                key_vectors,
                value_vectors,
                log_decay,
                write_strength,
                output_gate,
                norm_gain.reshape(1, N),
                out_proj,
            )
        )
    )


def solution(mesh):
    in_specs = (
        P("seq", "head"),
        P("seq", "head"),
        P("seq", "head"),
        P("head", "seq"),
        P("head", "seq"),
        P("seq", "head"),
        P(),
        P("head", None),
    )
    out_specs = P(("seq", "head"), None)
    return jax.shard_map(
        on_device, mesh=mesh, in_specs=in_specs, out_specs=out_specs, check_vma=False
    )
```

```python
import jax
import jax.numpy as jnp
from jax import lax
from jax.experimental import pallas as pl
from jax.experimental.pallas import tpu as pltpu
from jax.sharding import PartitionSpec as P

MESH = pl.DeviceIdType.MESH
F32 = jnp.float32
BF16 = jnp.bfloat16

GROUP = 16
GROUPS = 4
CHIPS = GROUP // 2
SIDE = 4
HALVES = 2
HALF = CHIPS // HALVES
FANS = 4
HEADS = 8
SHARE = HEADS // 2
N = 128
GROWS = 16
MSG = GROWS + 2 * N
CHUNKS = 6
EPS = 1e-06
OWNERS = tuple(
    2 * (SIDE * ((h + h // SHARE + 1) % 2) + h % SHARE) + h // SHARE for h in range(HEADS)
)
FARTHEST = (2, 6, 1, 3, 5, 7, 4)


def bdot(left, right, dims):
    return lax.dot_general(
        left.astype(BF16), right.astype(BF16), (dims, ((0,), (0,))), preferred_element_type=F32
    )


NN = ((2,), (1,))
NT = ((2,), (2,))
TN = ((1,), (1,))


def split(x):
    high = x.astype(BF16)
    return high, (x - high.astype(F32)).astype(BF16)


def bdot_left(left, right):
    return bdot(jnp.concatenate(split(left), axis=2), jnp.concatenate([right, right], axis=1), NN)


def bdot_right_turned(left, right):
    return bdot(
        jnp.concatenate([left, left], axis=1), jnp.concatenate(split(right), axis=1), TN
    )


def bdot_both(left, right):
    lh, ll = split(left)
    rh, rl = split(right)
    return bdot(
        jnp.concatenate([lh, ll, lh], axis=2), jnp.concatenate([rh, rh, rl], axis=1), NN
    )


def dot(left, right):
    return jnp.dot(left.astype(BF16), right.astype(BF16), preferred_element_type=F32)


def dot_turned(left, right):
    return lax.dot_general(
        left.astype(BF16), right.astype(BF16), (((1,), (1,)), ((), ())), preferred_element_type=F32
    )


def thirds(x):
    high = x.astype(BF16)
    rest = x - high.astype(F32)
    middle = rest.astype(BF16)
    return high, middle, (rest - middle.astype(F32)).astype(BF16)


def dot_right(left, right):
    return dot(jnp.concatenate([left, left], axis=1), jnp.concatenate(split(right), axis=0))


def dot_both(left, right):
    lh, ll = split(left)
    rh, rl = split(right)
    return dot(jnp.concatenate([lh, ll, lh], axis=1), jnp.concatenate([rh, rh, rl], axis=0))


def places():
    shape = (1, N, N)
    return lax.broadcasted_iota(jnp.int32, shape, 1), lax.broadcasted_iota(jnp.int32, shape, 2)


def mask(where):
    return jnp.where(where, 1.0, 0.0).astype(F32)


def inverse(couple):
    row, col = places()

    def between(size, count):
        return mask(
            ((row // (count * size)) == (col // (count * size))) & ((row // size) > (col // size))
        )

    eye = mask(row == col)
    solved = eye - couple * between(1, 2)
    size = 2
    while size < N:
        near = solved.astype(BF16)
        step = bdot(near, couple * between(size, 4), NN).astype(BF16)
        prod = bdot(step, jnp.concatenate([step, near], axis=2), NN)
        solved = solved - prod[:, :, N:]
        solved = solved + bdot(prod[:, :, :N], solved, NN)
        size *= 4
    near = solved.astype(BF16)
    solved = near.astype(F32)
    rest = (eye - solved) - bdot_left(couple, near)
    return solved + bdot(near, rest, NN)


def local_solve(keyrow, cum_row, cum_col, str_row, str_col):
    row, col = places()
    keykey = bdot(keyrow, keyrow, NT)
    diag = keykey * mask(row == col)
    kscale_row = lax.rsqrt(jnp.sum(diag, axis=1, keepdims=True) + EPS)
    kscale_col = lax.rsqrt(jnp.sum(diag, axis=2, keepdims=True) + EPS)
    ratio = jnp.exp(jnp.minimum(cum_col - cum_row, 0.0)) * mask(row >= col) * kscale_row
    couple = ratio * keykey * mask(row > col) * (str_col * kscale_col)
    solved = inverse(couple)
    last = cum_row[:, :, N - 1 :]
    return (
        solved * (str_row * jnp.exp(cum_row) * kscale_row),
        solved * str_row,
        ratio,
        jnp.exp(last - cum_col) * kscale_col,
        jnp.exp(last),
    )


def local_ends(keyrow, value, for_key, for_value, tail):
    both = jnp.concatenate([bdot_left(for_key, keyrow), bdot_left(for_value, value)], axis=2)
    return both, bdot_right_turned(keyrow, both * tail)


def local_reads(query, keyrow, ratio, both, cum_col):
    query32 = query.astype(F32)
    qscale = lax.rsqrt(jnp.sum(query32 * query32, axis=2, keepdims=True) + EPS)
    score = ratio * bdot(query, keyrow, NT) * qscale
    read = bdot_both(score, both)
    reach = query32 * (jnp.exp(cum_col) * qscale) - read[:, :, :N]
    return reach, read[:, :, N:]


def decay_rows(gain):
    place = lax.broadcasted_iota(jnp.int32, gain.shape, gain.ndim - 2)
    high = gain.astype(BF16).astype(F32)
    middle = (gain - high).astype(BF16).astype(F32)
    low = gain - high - middle
    rows = jnp.where(place == 0, high, jnp.where(place == 1, middle, jnp.where(place == 2, low, 0.0)))
    return rows.astype(BF16)


def read_message(message):
    gain = jnp.sum(message[..., N : N + GROWS, :].astype(F32), axis=-2, keepdims=True)
    return gain, message[..., N + GROWS :, :], message[..., :N, :]


def advance(run, step):
    run_g, run_d, run_j = run
    step_g, step_d, step_j = step
    prod = dot_right(step_d, jnp.concatenate([run_d, run_j], axis=1))
    return (
        run_g * step_g,
        step_g * run_d + run_g * step_d.astype(F32) + prod[:, :N],
        step_g * run_j + step_j.astype(F32) + prod[:, N:],
    )


def join(run, step):
    run_g, run_d, run_j = run
    step_g, step_d, step_j = step
    prod = dot_both(step_d, jnp.concatenate([run_d, run_j], axis=1))
    return (
        run_g * step_g,
        step_g * run_d + run_g * step_d + prod[:, :N],
        step_g * run_j + step_j + prod[:, N:],
    )


def kernel(
    q_any,
    k_any,
    v_any,
    decay_any,
    strength_any,
    gate_any,
    gain_any,
    proj_any,
    out_ref,
    q_buf,
    k_buf,
    v_buf,
    decay_buf,
    strength_buf,
    gate_buf,
    gain_buf,
    proj_buf,
    terms,
    chip_send,
    chip_recv,
    pre_d,
    pre_j,
    pre_g,
    total_buf,
    state_buf,
    state_send,
    state_recv,
    reach_buf,
    local_buf,
    normed_buf,
    share_buf,
    part_buf,
    sum_buf,
    part_recv,
    load_sem,
    xs_sem,
    xr_sem,
    cs_sem,
    cr_sem,
    ts_sem,
    tr_sem,
    ss_sem,
    sr_sem,
    ps_sem,
    pr_sem,
):
    place = lax.axis_index("seq")
    fan = lax.axis_index("head")
    group = place // GROUP
    mine = lax.rem(place, GROUP)
    base = group * GROUP
    core = lax.rem(mine, 2)
    chip = mine // 2
    side = lax.rem(chip, SIDE)
    partner = place + 1 - 2 * core
    first_head = core * SHARE
    owner = chip // SIDE == lax.rem(side + core + 1, 2)
    own_head = first_head + side
    peers = [lax.rem(mine + step, GROUP) for step in range(1, GROUP)]
    ahead = lax.rem(fan + 1 + 2 * core, FANS)
    behind = lax.rem(fan + 3 - 2 * core, FANS)
    opposite = lax.rem(fan + 2, FANS)

    loads = [
        pltpu.make_async_copy(source, target, load_sem.at[n])
        for n, (source, target) in enumerate(
            (
                (decay_any, decay_buf),
                (strength_any, strength_buf),
                (k_any, k_buf),
                (v_any, v_buf),
                (q_any, q_buf),
                (gate_any, gate_buf),
                (gain_any, gain_buf),
                (proj_any, proj_buf),
            )
        )
    ]
    for load in loads:
        load.start()

    barrier = pltpu.get_barrier_semaphore()
    greeted = [(base + peer, fan) for peer in peers]
    greeted += [(lax.rem(place + step * GROUP, GROUPS * GROUP), fan) for step in range(1, GROUPS)]
    greeted += [(place, ahead), (place, behind)]
    for device in greeted:
        pl.semaphore_signal(barrier, inc=1, device_id=device, device_id_type=MESH)

    def remote(source, target, send, recv, device):
        return pltpu.make_async_remote_copy(
            src_ref=source,
            dst_ref=target,
            send_sem=send,
            recv_sem=recv,
            device_id=device,
            device_id_type=MESH,
        )

    def pair_copy(half, sender):
        part = terms.at[sender, pl.ds(half * SHARE, SHARE)]
        return remote(part, part, xs_sem.at[half], xr_sem.at[half], (partner, fan))

    def owner_chip(n):
        return SIDE * lax.rem(n + core + 1, 2) + n

    def chip_copy(n, sender):
        return remote(
            chip_send.at[n],
            chip_recv.at[sender],
            cs_sem.at[n],
            cr_sem.at[sender],
            (base + 2 * owner_chip(n) + core, fan),
        )

    def total_copy(source, target):
        rows = N if source == 0 else MSG
        return remote(
            total_buf.at[source, pl.ds(0, rows)],
            total_buf.at[source, pl.ds(0, rows)],
            ts_sem.at[target],
            tr_sem.at[source],
            (target * GROUP + mine, fan),
        )

    def state_copy(at, side_core):
        return remote(
            state_send.at[at],
            state_recv.at[own_head],
            ss_sem.at[at, side_core],
            sr_sem.at[own_head],
            (base + 2 * at + side_core, fan),
        )

    def state_copies():
        for step in FARTHEST:
            for side_core in range(2):
                yield state_copy(lax.rem(chip + step, CHIPS), side_core)
        yield state_copy(chip, 1 - core)

    for load in loads[:3]:
        load.wait()
    row, col = places()
    below = mask(row[0] >= col[0])
    decays, strengths = thirds(decay_buf[...]), thirds(strength_buf[...])
    cumul = sum(dot_turned(third, below) for third in decays)
    cumul_turned = sum(dot_turned(below, third) for third in decays)
    strength = strength_buf[...]
    strength_turned = sum(dot_turned(mask(row[0] == col[0]), third) for third in strengths)
    heads = range(HEADS)
    cum_row = jnp.stack([cumul[h : h + 1, :] for h in heads])
    str_row = jnp.stack([strength[h : h + 1, :] for h in heads])
    cum_col = jnp.stack([cumul_turned[:, h : h + 1] for h in heads])
    str_col = jnp.stack([strength_turned[:, h : h + 1] for h in heads])

    def per_head(buf):
        return jnp.stack([buf[:, h * N : (h + 1) * N] for h in heads])

    keyrow = per_head(k_buf)
    for_key, for_value, ratio, tail, last = local_solve(keyrow, cum_row, cum_col, str_row, str_col)
    loads[3].wait()
    both, ends = local_ends(keyrow, per_head(v_buf), for_key, for_value, tail)
    own = terms.at[core]
    own[:, :N, :] = ends[:, :, N:].astype(BF16)
    own[:, N : N + GROWS, :] = decay_rows(jnp.broadcast_to(last, (HEADS, GROWS, N)))
    own[:, N + GROWS :, :] = (-ends[:, :, :N]).astype(BF16)

    pl.semaphore_wait(barrier, len(greeted))
    pair_copy(1 - core, core).start()

    @pl.when(core == 0)
    def _():
        pair_copy(0, core).start()

    pair_copy(core, 1 - core).wait_recv()
    share = pl.ds(first_head, SHARE)
    first_g, first_d, first_j = read_message(terms[0, share])
    second_g, second_d, second_j = read_message(terms[1, share])
    prod = bdot(second_d, jnp.concatenate([first_d, first_j], axis=2), NN)
    first_d, first_j, second_d, second_j = (
        x.astype(F32) for x in (first_d, first_j, second_d, second_j)
    )
    chip_send[:, :N, :] = (second_g * first_j + second_j + prod[:, :, N:]).astype(BF16)
    chip_send[:, N : N + GROWS, :] = decay_rows(
        jnp.broadcast_to(first_g * second_g, (SHARE, GROWS, N))
    )
    chip_send[:, N + GROWS :, :] = (
        second_g * first_d + first_g * second_d + prod[:, :, :N]
    ).astype(BF16)

    for step in (2, 1, 3):
        chip_copy(lax.rem(side + step, SIDE), chip).start()

    @pl.when(jnp.logical_not(owner))
    def _():
        chip_copy(side, chip).start()

    loads[4].wait()
    reach, local = local_reads(per_head(q_buf), keyrow, ratio, both, cum_col)
    reach_buf[...] = reach
    local_buf[...] = local

    @pl.when(core == 1)
    def _():
        pair_copy(0, 0).wait_recv()
        before_g, before_d, before_j = read_message(terms[0])
        prod = bdot_left(reach_buf[...], jnp.concatenate([before_d, before_j], axis=2))
        reach_buf[...] = before_g * reach_buf[...] + prod[:, :, :N]
        local_buf[...] = local_buf[...] + prod[:, :, N:]

    @pl.when(owner)
    def _():
        chip_recv[chip] = chip_send[side]
        runs = [None] * HALVES
        for i in range(HALF):
            for n in range(HALVES):
                at = n * HALF + i

                @pl.when(chip != at)
                def _():
                    chip_copy(0, at).wait_recv()

            for n in range(HALVES):
                at = n * HALF + i
                step = read_message(chip_recv[at])
                if i == 0:
                    pre_g[at] = jnp.ones((8, N), F32)
                    pre_d[pl.ds(at * N, N), :] = jnp.zeros((N, N), BF16)
                    pre_j[at] = jnp.zeros((N, N), F32)
                    runs[n] = (step[0], step[1].astype(F32), step[2].astype(F32))
                else:
                    run_g, run_d, run_j = runs[n]
                    pre_g[at] = jnp.broadcast_to(run_g, (8, N))
                    pre_d[pl.ds(at * N, N), :] = run_d.astype(BF16)
                    pre_j[at] = run_j
                    runs[n] = advance(runs[n], step)
        total_g, total_d, total_j = join(runs[0], runs[1])
        total_buf[group, :N, :] = total_j.astype(BF16)
        total_buf[group, N : N + GROWS, :] = decay_rows(jnp.broadcast_to(total_g, (GROWS, N)))
        total_buf[group, N + GROWS :, :] = total_d.astype(BF16)

        for source in range(GROUPS - 1):

            @pl.when(group == source)
            def _():
                for target in reversed(range(source + 1, GROUPS)):
                    total_copy(source, target).start()

        before_g, before_d, before_j = runs[0]
        prod = dot_right(pre_d[HALF * N :, :], jnp.concatenate([before_d, before_j], axis=1))
        for i in range(HALF):
            at = HALF + i
            lines = slice(i * N, (i + 1) * N)
            gain = pre_g[at, :1, :]
            own_d = pre_d[at * N : (at + 1) * N, :].astype(F32)
            pre_j[at] = gain * before_j + pre_j[at] + prod[lines, N:]
            pre_d[at * N : (at + 1) * N, :] = (
                gain * before_d + before_g * own_d + prod[lines, :N]
            ).astype(BF16)
            pre_g[at] = jnp.broadcast_to(gain * before_g, (8, N))

        state_buf[...] = jnp.zeros((N, N), F32)
        for source in range(GROUPS - 1):

            @pl.when(group > source)
            def _():
                total_copy(source, source + 1).wait_recv()
                if source == 0:
                    state_buf[...] = total_buf[0, :N, :].astype(F32)
                else:
                    gain, step_d, step_j = read_message(total_buf[source])
                    state = state_buf[...]
                    state_buf[...] = (
                        gain * state + dot_right(step_d, state) + step_j.astype(F32)
                    )

        state = state_buf[...]
        moved = dot(pre_d[...], state).reshape(CHIPS, N, N) + pre_j[...]
        state_send[...] = (moved + pre_g[:, :1, :] * state).astype(BF16)
        for copy in state_copies():
            copy.start()
        state_recv[own_head] = state_send[chip]

    loads[5].wait()
    loads[6].wait()
    gating = jax.nn.sigmoid(gate_buf[...].astype(F32)) * jnp.tile(gain_buf[...], (1, HEADS))
    for h in range(HEADS):

        @pl.when(mine != OWNERS[h])
        def _():
            remote(
                state_send.at[h],
                state_recv.at[h],
                ss_sem.at[h, 0],
                sr_sem.at[h],
                (base + OWNERS[h], fan),
            ).wait_recv()

    outputs = bdot_left(reach_buf[...], state_recv[...]) + local_buf[...]
    square = jnp.mean(outputs * outputs, axis=2, keepdims=True)
    outputs = outputs * lax.rsqrt(square + EPS)
    for h in range(HEADS):
        columns = slice(h * N, (h + 1) * N)
        normed_buf[:, columns] = (outputs[h] * gating[:, columns]).astype(BF16)

    loads[7].wait()
    rows = N // FANS
    width = proj_buf.shape[1] // CHUNKS

    def lines(owner_fan):
        return pl.ds(pl.multiple_of(owner_fan * rows, rows), rows)

    def part_copy(c, kind):
        source, to = (
            (part_buf.at[c, lines(opposite)], ahead),
            (part_buf.at[c, lines(behind)], behind),
            (sum_buf.at[c], ahead),
        )[kind]
        return remote(
            source, part_recv.at[c, kind], ps_sem.at[c, kind], pr_sem.at[c, kind], (place, to)
        )

    for c in range(CHUNKS):
        share = jnp.dot(
            normed_buf[...],
            proj_buf[:, c * width : (c + 1) * width],
            preferred_element_type=F32,
        )
        part_buf[c] = share.astype(BF16)
        part_copy(c, 0).start()
        share_buf[c] = share
    for c in range(CHUNKS):
        part_copy(c, 1).start()
    for c in range(CHUNKS):
        part_copy(c, 0).wait_recv()
        summed = share_buf[c, lines(ahead)] + part_recv[c, 0].astype(F32)
        sum_buf[c] = summed.astype(BF16)
        part_copy(c, 2).start()
    for c in range(CHUNKS):
        part_copy(c, 1).wait_recv()
        part_copy(c, 2).wait_recv()
        summed = share_buf[c, lines(fan)] + part_recv[c, 1].astype(F32)
        summed = summed + part_recv[c, 2].astype(F32)
        out_ref[:, c * width : (c + 1) * width] = summed.astype(BF16)

    pair_copy(1 - core, core).wait_send()

    @pl.when(core == 0)
    def _():
        pair_copy(0, core).wait_send()

    for n in range(SHARE):

        @pl.when(chip != owner_chip(n))
        def _():
            chip_copy(n, chip).wait_send()

    @pl.when(owner)
    def _():
        for source in range(GROUPS - 1):

            @pl.when(group == source)
            def _():
                for target in range(source + 1, GROUPS):
                    total_copy(source, target).wait_send()

        for copy in state_copies():
            copy.wait_send()

    for c in range(CHUNKS):
        for kind in range(3):
            part_copy(c, kind).wait_send()


def on_device(
    query_vectors,
    key_vectors,
    value_vectors,
    log_decay,
    write_strength,
    output_gate,
    norm_gain,
    out_proj,
):
    rows, wide = query_vectors.shape
    depth, width = out_proj.shape
    dma = pltpu.SemaphoreType.DMA
    return pl.pallas_call(
        kernel,
        out_shape=jax.ShapeDtypeStruct((rows // FANS, width), BF16),
        in_specs=[pl.BlockSpec(memory_space=pltpu.HBM)] * 8,
        out_specs=pl.BlockSpec(memory_space=pltpu.VMEM),
        scratch_shapes=[
            pltpu.VMEM((rows, wide), BF16),
            pltpu.VMEM((rows, wide), BF16),
            pltpu.VMEM((rows, wide), BF16),
            pltpu.VMEM((HEADS, N), F32),
            pltpu.VMEM((HEADS, N), F32),
            pltpu.VMEM((rows, wide), BF16),
            pltpu.VMEM((1, N), F32),
            pltpu.VMEM((depth, width), BF16),
            pltpu.VMEM((2, HEADS, MSG, N), BF16),
            pltpu.VMEM((SHARE, MSG, N), BF16),
            pltpu.VMEM((CHIPS, MSG, N), BF16),
            pltpu.VMEM((CHIPS * N, N), BF16),
            pltpu.VMEM((CHIPS, N, N), F32),
            pltpu.VMEM((CHIPS, 8, N), F32),
            pltpu.VMEM((GROUPS, MSG, N), BF16),
            pltpu.VMEM((N, N), F32),
            pltpu.VMEM((CHIPS, N, N), BF16),
            pltpu.VMEM((HEADS, N, N), BF16),
            pltpu.VMEM((HEADS, N, N), F32),
            pltpu.VMEM((HEADS, N, N), F32),
            pltpu.VMEM((rows, wide), BF16),
            pltpu.VMEM((CHUNKS, rows, width // CHUNKS), F32),
            pltpu.VMEM((CHUNKS, rows, width // CHUNKS), BF16),
            pltpu.VMEM((CHUNKS, rows // FANS, width // CHUNKS), BF16),
            pltpu.VMEM((CHUNKS, 3, rows // FANS, width // CHUNKS), BF16),
            dma((8,)),
            dma((2,)),
            dma((2,)),
            dma((SHARE,)),
            dma((CHIPS,)),
            dma((GROUPS,)),
            dma((GROUPS,)),
            dma((CHIPS, 2)),
            dma((HEADS,)),
            dma((CHUNKS, 3)),
            dma((CHUNKS, 3)),
        ],
        compiler_params=pltpu.CompilerParams(
            collective_id=0, has_side_effects=True, vmem_limit_bytes=48 * 1024 * 1024
        ),
        cost_estimate=pl.CostEstimate(
            flops=2_000_000_000, bytes_accessed=6_000_000, transcendentals=500_000
        ),
    )(
        *(
            pltpu.with_memory_space_constraint(array, pltpu.HBM)
            for array in (
                query_vectors,
                key_vectors,
                value_vectors,
                log_decay,
                write_strength,
                output_gate,
                norm_gain.reshape(1, N),
                out_proj,
            )
        )
    )


def solution(mesh):
    in_specs = (
        P("seq", "head"),
        P("seq", "head"),
        P("seq", "head"),
        P("head", "seq"),
        P("head", "seq"),
        P("seq", "head"),
        P(),
        P("head", None),
    )
    out_specs = P(("seq", "head"), None)
    return jax.shard_map(
        on_device, mesh=mesh, in_specs=in_specs, out_specs=out_specs, check_vma=False
    )
```
